32 devices in a mesh: row: 4 (over y, core), col: 2 (over x), layer: 4 (over z).
Axes of the slice: x: 2, y: 2, z: 4, core: 2. Of those that a mesh axis runs over, the one named last changes fastest.
Arguments:
- blocks: bfloat16 [704, 128, 128], P(('col', 'layer')), may hold values from -6 to 6
- block_aux: int32 [704], P(('col', 'layer')), may hold values from 0 to 23
- block_row: int32 [704], P(('col', 'layer')), may hold values from 0 to 1, as said below
- block_col: int32 [704], P(('col', 'layer')), may hold values from 0 to 159, as said below
- extents: int32 [704], P(('col', 'layer')), may hold values from 32 to 128
- occ_green: bfloat16 [20480, 256], P('layer', 'row'), may hold values from -0.01171875 to 0.01171875
- virt_green: bfloat16 [20480, 256], P('layer', 'row'), may hold values from -0.01171875 to 0.01171875
Outputs:
- chi: float32 [24, 24], replicated
The draws below stay inside these ranges and needn't reach their ends.
Inputs may be any that keep to these rules, and one draw needn't show every extreme that they name: block_row[n] numbers the block of 128 window functions that tile n covers. The owner of tile n is the pair (block_row[n], block_col[n] // 40). Within each device's share of 88 consecutive entries no owner appears more than 12 times, and one owner, the same for every share, appears exactly 12 times in every share.
All inputs are finite; a program needn't handle non-finite values.
Results may differ from the reference program's by a relative error of at most 0.0003.
Values may be sent and summed in bfloat16 or wider, within the bound.
A program may use at most 192 MiB of HBM per device.

```python
import jax
import jax.numpy as jnp
from jax import lax

NP = 24
BS = 128
NB = 20480
BLK_DEV = 88
W = 256
KQ = 40
DESTS = 8
CAP = 12
NBLK = 704
N_LAYER = 4


def pick_owners(key):
    base_key = jax.random.fold_in(key, 11)
    star_key, order_key, column_key = jax.random.split(base_key, 3)
    busiest = jax.random.randint(star_key, (), 0, DESTS).astype(jnp.int32)
    pool_size = (DESTS - 1) * CAP

    def one_share(share_key):
        pick_key, shuffle_key = jax.random.split(share_key)
        picks = jax.random.permutation(pick_key, pool_size)[:BLK_DEV - CAP].astype(jnp.int32)
        others = picks // CAP
        others = others + (others >= busiest).astype(jnp.int32)
        owners = jnp.concatenate([jnp.full((CAP,), busiest, jnp.int32), others])
        return owners[jax.random.permutation(shuffle_key, BLK_DEV)]
    owners = jax.vmap(one_share)(jax.random.split(order_key, DESTS)).reshape(-1)
    window_block = owners // N_LAYER
    basis_block = owners % N_LAYER * KQ + jax.random.randint(column_key, (NBLK,), 0, KQ).astype(jnp.int32)
    return (window_block.astype(jnp.int32), basis_block.astype(jnp.int32))


def draw_block_row(key, part):
    return pick_owners(key)[0]


def draw_block_col(key, part):
    return pick_owners(key)[1]


def set_ends(entries, rng, low, largest):
    dims = entries.shape
    place = [jax.random.randint(jax.random.fold_in(rng, axis), (), 0, dims[axis]) for axis in range(len(dims))]
    entries = entries.at[tuple(place)].set(low)
    longest = dims.index(max(dims))
    place[longest] = (place[longest] + 1) % dims[longest]
    return entries.at[tuple(place)].set(largest)


def block_levels(rng, extent, pieces, smallest, top_value):
    gain, own = 1.0, jax.random.fold_in(rng, 6)
    for dim, blocks in pieces:
        steps = jnp.exp(jax.random.uniform(jax.random.fold_in(own, dim), (blocks,), jnp.float32, smallest / len(pieces), top_value / len(pieces)))
        gain = gain * jnp.repeat(steps, extent[dim] // blocks).reshape([-1 if axis == dim else 1 for axis in range(len(extent))])
    return gain


def bell_draw(key, shape, deviation, limit, shards=(), kind=jnp.bfloat16):
    level = block_levels(key, shape, shards, -0.22, 0.18) if shards else 1.0
    values = jax.random.normal(key, shape, jnp.float32) * deviation * level
    return jnp.minimum(jnp.maximum(values, -limit), limit).astype(kind)


def setup_inputs(seed: int = 0) -> dict:
    arg_keys = jax.random.split(jax.random.key(seed), 8)
    return {
        "blocks": bell_draw(arg_keys[0], (NBLK, BS, BS), 1.0, 6.0, ((0, 8),)),
        "block_aux": set_ends(jax.random.randint(arg_keys[1], (NBLK,), 0, NP), jax.random.fold_in(arg_keys[1], 1), 0, NP - 1).astype(jnp.int32),
        "block_row": draw_block_row(jax.random.fold_in(arg_keys[7], 71), 0),
        "block_col": draw_block_col(jax.random.fold_in(arg_keys[7], 71), 0),
        "extents": set_ends(jax.random.randint(arg_keys[4], (NBLK,), BS // 4, BS + 1), jax.random.fold_in(arg_keys[4], 1), BS // 4, BS).astype(jnp.int32),
        "occ_green": bell_draw(arg_keys[5], (NB, W), (5 * BS * BS * NBLK // (8 * NP)) ** -0.5, 0.01171875, ((0, 4), (1, 4))),
        "virt_green": bell_draw(arg_keys[6], (NB, W), (5 * BS * BS * NBLK // (8 * NP)) ** -0.5, 0.01171875, ((0, 4), (1, 4))),
    }


def reference(blocks, block_aux, block_row, block_col, extents, occ_green, virt_green):
    columns = jnp.arange(BS, dtype=jnp.int32)
    masked_tiles = jnp.where(columns[None, None, :] < extents[:, None, None], blocks, jnp.zeros((), blocks.dtype))
    anchor = jnp.zeros((), jnp.int32)

    def add_block(totals, record):
        occ_part, virt_part = totals
        one_tile, aux_index, row_block, col_block = record
        basis_start = (col_block * BS).astype(jnp.int32)
        window_start = (row_block * BS).astype(jnp.int32)
        occ_rows = lax.dynamic_slice_in_dim(occ_green, basis_start, BS, 0)
        virt_rows = lax.dynamic_slice_in_dim(virt_green, basis_start, BS, 0)
        occ_term = jnp.dot(one_tile, occ_rows, preferred_element_type=jnp.float32)
        virt_term = jnp.dot(one_tile, virt_rows, preferred_element_type=jnp.float32)
        where_to = (aux_index.astype(jnp.int32), window_start, anchor)
        occ_prior = lax.dynamic_slice(occ_part, where_to, (1, BS, W))
        virt_prior = lax.dynamic_slice(virt_part, where_to, (1, BS, W))
        occ_part = lax.dynamic_update_slice(occ_part, occ_prior + occ_term[None], where_to)
        virt_part = lax.dynamic_update_slice(virt_part, virt_prior + virt_term[None], where_to)
        return (occ_part, virt_part), None

    empty = jnp.zeros((NP, W, W), jnp.float32)
    (occ_part, virt_part), _ = lax.scan(add_block, (empty, empty), (masked_tiles, block_aux, block_row, block_col))
    return jnp.einsum("plv,qvl->pq", occ_part, virt_part, precision=lax.Precision.HIGHEST)
```

```python
import jax
import jax.numpy as jnp
from jax import lax
from jax.experimental import pallas as pl
from jax.experimental.pallas import tpu as pltpu
from jax.sharding import PartitionSpec as P

NP = 24
MESH = pl.DeviceIdType.MESH
VMEM_LIMIT = 40 * 1024 * 1024
OFFSETS = ((1, 2), (1, 1), (1, 3), (0, 2), (0, 1), (0, 3), (1, 0))


def slot_kernel(cap, layers, layer_blocks, aux_ref, row_ref, col_ref, ext_ref, pick_ref, meta_ref, count):
    held = aux_ref.shape[0]
    owners = meta_ref.shape[0]

    @pl.loop(0, owners)
    def _(o):
        count[o] = 0

        @pl.loop(0, cap)
        def _(j):
            pick_ref[0, o * cap + j] = 0
            pick_ref[1, o * cap + j] = 0
            meta_ref[o, 0, j] = 0

    @pl.loop(0, held)
    def _(n):
        block = col_ref[n]
        layer = block // layer_blocks
        owner = row_ref[n] * layers + layer
        rank = count[owner]
        count[owner] = rank + 1
        pick_ref[0, owner * cap + rank] = n
        pick_ref[1, owner * cap + rank] = ext_ref[n]
        meta_ref[owner, 0, rank] = aux_ref[n] * 256 + block - layer * layer_blocks


def place():
    row, col, layer = lax.axis_index("row"), lax.axis_index("col"), lax.axis_index("layer")
    return row // 2, row % 2, col, layer


def exchange_kernel(cap, pick_ref, meta_ref, blocks_ref, occ_ref, virt_ref, tiles_ref, meta_out, green_ref,
                    send_buf, green_in, meta_send, meta_recv, tile_send, tile_recv,
                    y_send, y_recv, core_send, core_recv, green_send, green_recv):
    y, core, col, layer = place()
    row = 2 * y + core
    across = 2 * (1 - y) + core
    sibling = 2 * y + 1 - core
    me = col * 4 + layer
    part = cap // 4
    side = blocks_ref.shape[1]

    barrier = pltpu.get_barrier_semaphore()
    peers = [(row, (col + dc) % 2, (layer + dl) % 4) for dc, dl in OFFSETS]
    for peer in peers + [(across, col, layer), (sibling, col, layer)]:
        pl.semaphore_signal(barrier, inc=1, device_id=peer, device_id_type=MESH)
    pl.semaphore_wait(barrier, len(peers) + 2)

    def greens(source):
        return pltpu.make_async_remote_copy(
            src_ref=source, dst_ref=green_in, send_sem=green_send, recv_sem=green_recv,
            device_id=(sibling, col, layer), device_id_type=MESH)

    @pl.when(core == 0)
    def _():
        greens(virt_ref).start()

    @pl.when(core == 1)
    def _():
        greens(occ_ref).start()

    lanes = lax.broadcasted_iota(jnp.int32, (side, side), 1)

    def packed(owner, j):
        slot = owner * cap + row * part + j
        tile = blocks_ref[pick_ref[0, slot]]
        return jnp.where(lanes < pick_ref[1, slot], tile.astype(jnp.float32), 0.0).astype(tile.dtype)

    first = []
    for k, peer in enumerate(peers):
        owner = peer[1] * 4 + peer[2]
        for j in range(part):
            send_buf[k, j] = packed(owner, j)
        tile_copy = pltpu.make_async_remote_copy(
            src_ref=send_buf.at[k], dst_ref=tiles_ref.at[row, me], send_sem=tile_send.at[k],
            recv_sem=tile_recv.at[k], device_id=peer, device_id_type=MESH)
        tile_copy.start()
        meta_copy = pltpu.make_async_remote_copy(
            src_ref=meta_ref.at[owner], dst_ref=meta_out.at[me], send_sem=meta_send.at[k],
            recv_sem=meta_recv.at[k], device_id=peer, device_id_type=MESH)
        meta_copy.start()
        first += [tile_copy, meta_copy]
    for j in range(part):
        tiles_ref[row, me, j] = packed(me, j)
    meta_out[me] = meta_ref[me]

    def forward(quarter, source, send, recv, k, target):
        copy = pltpu.make_async_remote_copy(
            src_ref=tiles_ref.at[quarter, source], dst_ref=tiles_ref.at[quarter, source],
            send_sem=send.at[k], recv_sem=recv.at[k], device_id=(target, col, layer), device_id_type=MESH)
        copy.start()
        return copy

    sources = [((col + dc) % 2) * 4 + (layer + 4 - dl) % 4 for dc, dl in OFFSETS] + [me]
    order = [7, 6, 4, 5, 1, 2, 3, 0]
    to_y, to_core = {}, {}
    for k in order:
        if k < 7:
            first[2 * k].wait_recv()
        to_y[k] = forward(row, sources[k], y_send, y_recv, k, across)
        to_core[k] = forward(row, sources[k], core_send, core_recv, k, sibling)

    greens(virt_ref).wait()
    half = green_in.shape[1]

    @pl.when(core == 0)
    def _():
        green_ref[:, :half] = occ_ref[...]
        green_ref[:, half:] = green_in[...]

    @pl.when(core == 1)
    def _():
        green_ref[:, :half] = green_in[...]
        green_ref[:, half:] = virt_ref[...]

    for k in order:
        to_y[k].wait_recv()
        to_core[8 + k] = forward(across, sources[k], core_send, core_recv, 8 + k, sibling)
    for k in range(7):
        first[2 * k].wait_send()
        first[2 * k + 1].wait()
    for k in order:
        to_y[k].wait_send()
        to_core[k].wait()
        to_core[8 + k].wait()


def product_kernel(cap, meta_ref, tiles_ref, green_ref, total_ref):
    part = cap // 4
    side = tiles_ref.shape[-1]
    total_ref[...] = jnp.zeros_like(total_ref)

    @pl.loop(0, tiles_ref.shape[0] * tiles_ref.shape[1] // 2)
    def _(i):
        terms = []
        for h in range(2):
            n = 2 * i + h
            quarter, source = n // tiles_ref.shape[1], n % tiles_ref.shape[1]
            for j in range(part):
                code = meta_ref[source, 0, quarter * part + j]
                start = pl.multiple_of((code % 256) * side, side)
                terms.append((code // 256, jnp.dot(tiles_ref[quarter, source, j], green_ref[pl.ds(start, side), :],
                                                   preferred_element_type=jnp.float32)))
        for aux, term in terms:
            total_ref[aux] += term

    @pl.when(lax.axis_index("row") % 2 == 1)
    def _():
        @pl.loop(0, total_ref.shape[0])
        def _(p):
            total_ref[p] = total_ref[p].T


def pair_kernel(total_ref, chi_ref, occ_in, virt_in, chi_buf, chi_in, send_sem, occ_sem, virt_sem,
                chi_send, chi_recv):
    y, core, x, z = place()
    row = 2 * y + core
    rows = occ_in.shape[2]
    diagonal = x == y
    partners = [
        (2 * y + 1 - core, x, z), (2 * (1 - y) + core, x, z), (row, 1 - x, z),
        (row, x, z + 1 - 2 * (z % 2)), (row, x, (z + 2) % 4)]

    barrier = pltpu.get_barrier_semaphore()
    for peer in partners[1:3]:
        pl.semaphore_signal(barrier, inc=1, device_id=peer, device_id_type=MESH)
    for dz in range(4):
        for dk in range(2):
            if dz or dk:
                pl.semaphore_signal(barrier, inc=1, device_id=(2 * y + (core + dk) % 2, x, (z + dz) % 4),
                                    device_id_type=MESH)
    @pl.when(jnp.logical_not(diagonal))
    def _():
        for dz in range(4):
            for dk in range(2):
                pl.semaphore_signal(barrier, inc=1, device_id=(2 * x + (core + dk) % 2, y, (z + dz) % 4),
                                    device_id_type=MESH)

    pl.semaphore_wait(barrier, 9 + 8 * (x - y) * (x - y))

    def part_of(kk, zz):
        return total_ref.at[:, pl.ds(pl.multiple_of((2 * zz + kk) * rows, rows), rows), :]

    def remote(into, sem, chip, kk, dz):
        zz = (z + dz) % 4
        return pltpu.make_async_remote_copy(
            src_ref=part_of(kk, zz), dst_ref=into.at[dz], send_sem=send_sem.at[dz * 2 + kk], recv_sem=sem.at[dz],
            device_id=(2 * chip[1] + kk, chip[0], zz), device_id_type=MESH)

    def local(into, sem):
        return pltpu.make_async_copy(part_of(core, z), into.at[0], sem.at[0])

    here, there = (x, y), (y, x)
    alone = jnp.logical_and(diagonal, core == 1)
    far_first = (2, 1, 3, 0)

    @pl.when(core == 0)
    def _():
        for dz in far_first:
            for kk in (1, 0):
                if dz == 0 and kk == 0:
                    local(occ_in, occ_sem).start()
                else:
                    remote(occ_in, occ_sem, here, kk, dz).start()

    @pl.when(core == 1)
    def _():
        for dz in far_first:
            for kk in (0, 1):
                if dz == 0 and kk == 1:
                    @pl.when(diagonal)
                    def _():
                        local(virt_in, virt_sem).start()

                    @pl.when(jnp.logical_not(diagonal))
                    def _():
                        remote(virt_in, virt_sem, there, kk, dz).start()
                else:
                    remote(virt_in, virt_sem, there, kk, dz).start()

    for dz in (0, 1, 3, 2):
        if dz:
            remote(occ_in, occ_sem, here, 0, dz).wait_recv()
            remote(virt_in, virt_sem, there, 1, dz).wait_recv()
        else:
            @pl.when(core == 0)
            def _():
                local(occ_in, occ_sem).wait()

            @pl.when(core == 1)
            def _():
                remote(occ_in, occ_sem, here, 0, 0).wait_recv()

            @pl.when(alone)
            def _():
                local(virt_in, virt_sem).wait()

            @pl.when(jnp.logical_not(alone))
            def _():
                remote(virt_in, virt_sem, there, 1, 0).wait_recv()

    occ_in[0] = (occ_in[0] + occ_in[1]) + (occ_in[2] + occ_in[3])
    virt_in[0] = (virt_in[0] + virt_in[1]) + (virt_in[2] + virt_in[3])
    count = total_ref.shape[0]
    chi = jnp.zeros((count, count), jnp.float32)
    for i in range(0, rows, 2):
        left = jnp.concatenate([occ_in[0, :, i, :], occ_in[0, :, i + 1, :]], axis=1)
        right = jnp.concatenate([virt_in[0, :, i, :], virt_in[0, :, i + 1, :]], axis=1)
        chi += lax.dot_general(left, right, (((1,), (1,)), ((), ())), precision=lax.Precision.HIGHEST,
                               preferred_element_type=jnp.float32)
    chi_buf[...] = jnp.zeros_like(chi_buf)
    chi_buf[0, :, :count] = chi

    for k, partner in enumerate(partners):
        copy = pltpu.make_async_remote_copy(
            src_ref=chi_buf.at[k], dst_ref=chi_in.at[k], send_sem=chi_send.at[k], recv_sem=chi_recv.at[k],
            device_id=partner, device_id_type=MESH)
        copy.start()
        copy.wait()
        chi_buf[k + 1] = chi_buf[k] + chi_in[k]
    chi_ref[...] = chi_buf[len(partners), :, :count]

    @pl.when(core == 0)
    def _():
        for dz in far_first:
            for kk in (1, 0):
                if dz or kk:
                    remote(occ_in, occ_sem, here, kk, dz).wait_send()

    @pl.when(core == 1)
    def _():
        for dz in far_first:
            remote(virt_in, virt_sem, there, 0, dz).wait_send()
            if dz:
                remote(virt_in, virt_sem, there, 1, dz).wait_send()

        @pl.when(jnp.logical_not(diagonal))
        def _():
            remote(virt_in, virt_sem, there, 1, 0).wait_send()


def on_slice(blocks, block_aux, block_row, block_col, extents, occ_green, virt_green):
    held, side, _ = blocks.shape
    layers, owners = 4, 8
    cap = held // owners + 1
    depth, width = occ_green.shape
    smem, vmem = pl.BlockSpec(memory_space=pltpu.SMEM), pl.BlockSpec(memory_space=pltpu.VMEM)
    f32, i32 = jnp.float32, jnp.int32
    dma = pltpu.SemaphoreType.DMA

    def bind(kernel, *sizes):
        def run(*refs):
            kernel(*sizes, *refs)
        return run

    pick, meta = pl.pallas_call(
        bind(slot_kernel, cap, layers, depth // side),
        out_shape=(jax.ShapeDtypeStruct((2, 128), i32), jax.ShapeDtypeStruct((owners, 8, 128), i32)),
        in_specs=[smem] * 4,
        out_specs=(smem, smem),
        scratch_shapes=[pltpu.SMEM((owners,), i32)],
        name="slots",
    )(block_aux, block_row, block_col, extents)
    part = cap // 4
    tiles, meta, green = pl.pallas_call(
        bind(exchange_kernel, cap),
        out_shape=(
            jax.ShapeDtypeStruct((4, owners, part, side, side), blocks.dtype),
            jax.ShapeDtypeStruct((owners, 8, 128), i32),
            jax.ShapeDtypeStruct((depth, 2 * width), occ_green.dtype),
        ),
        in_specs=[smem, vmem, vmem, vmem, vmem],
        out_specs=(vmem, vmem, vmem),
        scratch_shapes=[
            pltpu.VMEM((7, part, side, side), blocks.dtype),
            pltpu.VMEM((depth, width), occ_green.dtype),
            dma((7,)), dma((7,)), dma((7,)), dma((7,)), dma((8,)), dma((8,)), dma((16,)), dma((16,)),
            dma(()), dma(()),
        ],
        compiler_params=pltpu.CompilerParams(collective_id=0, has_side_effects=True, vmem_limit_bytes=VMEM_LIMIT),
        name="exchange",
    )(pick, meta, blocks, occ_green, virt_green)
    total = pl.pallas_call(
        bind(product_kernel, cap),
        out_shape=jax.ShapeDtypeStruct((NP, side, 2 * width), f32),
        in_specs=[smem, vmem, vmem],
        out_specs=vmem,
        compiler_params=pltpu.CompilerParams(vmem_limit_bytes=VMEM_LIMIT),
        name="product",
    )(meta, tiles, green)
    thin = side // 8
    return pl.pallas_call(
        pair_kernel,
        out_shape=jax.ShapeDtypeStruct((NP, NP), f32),
        in_specs=[vmem],
        out_specs=vmem,
        scratch_shapes=[
            pltpu.VMEM((4, NP, thin, side), f32),
            pltpu.VMEM((4, NP, thin, side), f32),
            pltpu.VMEM((6, NP, 128), f32),
            pltpu.VMEM((5, NP, 128), f32),
            dma((8,)), dma((4,)), dma((4,)), dma((5,)), dma((5,)),
        ],
        compiler_params=pltpu.CompilerParams(collective_id=1, has_side_effects=True, vmem_limit_bytes=VMEM_LIMIT),
        name="pair",
    )(total)


def on_device(blocks, block_aux, block_row, block_col, extents, occ_green, virt_green):
    row_count = lax.axis_size("row")
    col_count = lax.axis_size("col")
    layer_count = lax.axis_size("layer")
    held_count = blocks.shape[0]
    tile_side = blocks.shape[1]
    aux_count = NP
    owner_count = col_count * layer_count
    capacity = max(2, held_count // owner_count + 1)
    layer_blocks = occ_green.shape[0] // tile_side
    columns = jnp.arange(tile_side, dtype=jnp.int32)
    masked_tiles = jnp.where(
        columns[None, None, :] < extents[:, None, None], blocks, jnp.zeros((), blocks.dtype)
    )
    layer_of = block_col // layer_blocks
    target = block_row * layer_count + layer_of
    kept_col = block_col - layer_of * layer_blocks
    marked = (target[:, None] == jnp.arange(owner_count, dtype=jnp.int32)[None, :]).astype(
        jnp.int32
    )
    earlier = jnp.cumsum(marked, axis=0) - marked
    placed = target * capacity + jnp.sum(earlier * marked, axis=1)
    send_tiles = (
        jnp.zeros((owner_count * capacity, tile_side, tile_side), blocks.dtype)
        .at[placed]
        .set(masked_tiles)
    )
    send_meta = (
        jnp.zeros((owner_count * capacity, 2), jnp.int32)
        .at[placed]
        .set(jnp.stack([block_aux, kept_col], axis=1))
    )
    send_tiles = send_tiles.reshape(col_count, layer_count, capacity, tile_side, tile_side)
    send_meta = send_meta.reshape(col_count, layer_count, capacity, 2)
    total_slots = col_count * layer_count * capacity
    got_tiles, got_meta = (
        lax.all_to_all(
            send_tiles.reshape(total_slots, tile_side, tile_side),
            ("col", "layer"),
            split_axis=0,
            concat_axis=0,
            tiled=True,
        ),
        lax.all_to_all(
            send_meta.reshape(total_slots, 2),
            ("col", "layer"),
            split_axis=0,
            concat_axis=0,
            tiled=True,
        ),
    )
    group_size = col_count * capacity
    got_tiles = got_tiles.reshape(layer_count, group_size, tile_side, tile_side)
    got_meta = got_meta.reshape(layer_count, group_size, 2)
    occ_cols, virt_cols = (occ_green, virt_green)
    width_here = occ_cols.shape[1]
    offsets = jnp.arange(tile_side, dtype=jnp.int32)

    def add_group(totals, record):
        occ_total, virt_total = totals
        tile_group, meta_group = record
        row_index = meta_group[:, 1][:, None] * tile_side + offsets[None, :]
        occ_rows = occ_cols[row_index]
        virt_rows = virt_cols[row_index]
        occ_term = jnp.einsum(
            "gsv,gls->gvl", occ_rows, tile_group, preferred_element_type=jnp.float32
        )
        virt_term = jnp.einsum(
            "gvs,gsl->gvl", tile_group, virt_rows, preferred_element_type=jnp.float32
        )
        aux_index = meta_group[:, 0]
        return (
            (occ_total.at[aux_index].add(occ_term), virt_total.at[aux_index].add(virt_term)),
            None,
        )

    start_totals = (
        jnp.zeros((aux_count, width_here, tile_side), jnp.float32),
        jnp.zeros((aux_count, tile_side, width_here), jnp.float32),
    )
    (occ_total, virt_total), _ = lax.scan(add_group, start_totals, (got_tiles, got_meta))
    occ_done, virt_done = (
        lax.psum_scatter(occ_total, "layer", scatter_dimension=1, tiled=True),
        lax.psum_scatter(virt_total, "layer", scatter_dimension=2, tiled=True),
    )
    mesh_count = row_count * layer_count
    thin_rows = tile_side // mesh_count
    stack_count = mesh_count // col_count
    narrow = occ_done.shape[1]
    occ_five = occ_done.reshape(aux_count, 1, col_count, thin_rows, tile_side)
    virt_five = virt_done.reshape(aux_count, stack_count, col_count, thin_rows, narrow)
    occ_moved, virt_moved = (
        lax.all_to_all(occ_five, "col", split_axis=2, concat_axis=1, tiled=True),
        lax.all_to_all(virt_five, "col", split_axis=2, concat_axis=1, tiled=True),
    )
    virt_four = virt_moved.reshape(aux_count, mesh_count, thin_rows, narrow)
    virt_back = lax.all_to_all(virt_four, ("row", "layer"), split_axis=1, concat_axis=3, tiled=True)
    occ_final = occ_moved.reshape(aux_count, col_count, thin_rows, tile_side)
    virt_final = virt_back.reshape(aux_count, thin_rows, col_count, tile_side)
    chi_part = jnp.einsum(
        "pcji,qjci->pq",
        occ_final,
        virt_final,
        precision=lax.Precision.HIGHEST,
        preferred_element_type=jnp.float32,
    )
    return lax.psum(chi_part, ("row", "col", "layer"))


def solution(mesh):
    in_specs = (
        P(("col", "layer"), None, None),
        P(("col", "layer")),
        P(("col", "layer")),
        P(("col", "layer")),
        P(("col", "layer")),
        P("layer", "row"),
        P("layer", "row"),
    )
    out_specs = P()
    side_of = (mesh.shape["row"], mesh.shape["col"], mesh.shape["layer"])
    return jax.shard_map(
        on_slice if side_of == (4, 2, 4) else on_device, mesh=mesh, in_specs=in_specs, out_specs=out_specs, check_vma=False
    )
```

```python
import jax
import jax.numpy as jnp
from jax import lax
from jax.experimental import pallas as pl
from jax.experimental.pallas import tpu as pltpu
from jax.sharding import PartitionSpec as P

NP = 24
MESH = pl.DeviceIdType.MESH
VMEM_LIMIT = 40 * 1024 * 1024
STEPS = 8
OFFSETS = ((1, 2), (1, 1), (1, 3), (0, 2), (0, 1), (0, 3), (1, 0))


def slot_kernel(cap, layers, layer_blocks, aux_ref, row_ref, col_ref, ext_ref, pick_ref, meta_ref):
    held = aux_ref.shape[0]
    owners = meta_ref.shape[0]
    for o in range(owners):
        for j in range(cap):
            pick_ref[o * cap + j] = 0
            meta_ref[o, 0, j] = 0

    def put(n, counts):
        block = col_ref[n]
        layer = jnp.int32(0)
        for edge in range(1, layers):
            layer += (block >= edge * layer_blocks).astype(jnp.int32)
        owner = row_ref[n] * layers + layer
        rank = lax.shift_right_logical(counts, 4 * owner) & 15
        pick_ref[owner * cap + rank] = n * 256 + ext_ref[n]
        meta_ref[owner, 0, rank] = aux_ref[n] * 256 + block - layer * layer_blocks
        return counts + lax.shift_left(jnp.int32(1), 4 * owner)

    lax.fori_loop(0, held, put, jnp.int32(0), unroll=8)


def place():
    row, col, layer = lax.axis_index("row"), lax.axis_index("col"), lax.axis_index("layer")
    return row // 2, row % 2, col, layer


def exchange_kernel(cap, pick_ref, meta_ref, blocks_ref, occ_ref, virt_ref, tiles_ref, meta_out, green_ref,
                    send_buf, meta_send, meta_recv, tile_send, tile_recv,
                    y_send, y_recv, core_send, core_recv, green_send, green_recv):
    y, core, col, layer = place()
    row = 2 * y + core
    across = 2 * (1 - y) + core
    sibling = 2 * y + 1 - core
    me = col * 4 + layer
    part = cap // 4
    side = blocks_ref.shape[1]

    barrier = pltpu.get_barrier_semaphore()
    peers = [(row, (col + dc) % 2, (layer + dl) % 4) for dc, dl in OFFSETS]
    for peer in peers + [(across, col, layer), (sibling, col, layer)]:
        pl.semaphore_signal(barrier, inc=1, device_id=peer, device_id_type=MESH)
    pl.semaphore_wait(barrier, len(peers) + 2)

    half = occ_ref.shape[0]
    own_rows = pl.ds(pl.multiple_of(core * half, half), half)

    def greens(source):
        return pltpu.make_async_remote_copy(
            src_ref=source, dst_ref=green_ref.at[own_rows], send_sem=green_send, recv_sem=green_recv,
            device_id=(sibling, col, layer), device_id_type=MESH)

    @pl.when(core == 0)
    def _():
        greens(virt_ref).start()
        green_ref[:half] = occ_ref[...]

    @pl.when(core == 1)
    def _():
        greens(occ_ref).start()
        green_ref[half:] = virt_ref[...]

    lanes = lax.broadcasted_iota(jnp.int32, (side, side), 1)

    def packed(owner, j):
        pick = pick_ref[owner * cap + row * part + j]
        tile = blocks_ref[pick // 256]
        return jnp.where(lanes < pick % 256, tile.astype(jnp.float32), 0.0).astype(tile.dtype)

    def forward(quarter, source, send, recv, k, target):
        copy = pltpu.make_async_remote_copy(
            src_ref=tiles_ref.at[quarter, source], dst_ref=tiles_ref.at[quarter, source],
            send_sem=send.at[k], recv_sem=recv.at[k], device_id=(target, col, layer), device_id_type=MESH)
        copy.start()
        return copy

    sources = [((col + dc) % 2) * 4 + (layer + 4 - dl) % 4 for dc, dl in OFFSETS] + [me]
    order = [7, 6, 4, 5, 1, 2, 3, 0]
    to_y, to_core = {}, {}
    for j in range(part):
        tiles_ref[row, me, j] = packed(me, j)
    to_y[7] = forward(row, me, y_send, y_recv, 7, across)
    to_core[7] = forward(row, me, core_send, core_recv, 7, sibling)
    meta_out[me] = meta_ref[me]
    first = []
    for k, peer in enumerate(peers):
        owner = peer[1] * 4 + peer[2]
        for j in range(part):
            send_buf[k, j] = packed(owner, j)
        tile_copy = pltpu.make_async_remote_copy(
            src_ref=send_buf.at[k], dst_ref=tiles_ref.at[row, me], send_sem=tile_send.at[k],
            recv_sem=tile_recv.at[k], device_id=peer, device_id_type=MESH)
        tile_copy.start()
        meta_copy = pltpu.make_async_remote_copy(
            src_ref=meta_ref.at[owner], dst_ref=meta_out.at[me], send_sem=meta_send.at[k],
            recv_sem=meta_recv.at[k], device_id=peer, device_id_type=MESH)
        meta_copy.start()
        first += [tile_copy, meta_copy]

    for k in order:
        if k == 7:
            continue
        first[2 * k].wait_recv()
        to_y[k] = forward(row, sources[k], y_send, y_recv, k, across)
        to_core[k] = forward(row, sources[k], core_send, core_recv, k, sibling)

    greens(virt_ref).wait()
    for k in order:
        to_y[k].wait_recv()
        to_core[8 + k] = forward(across, sources[k], core_send, core_recv, 8 + k, sibling)
    for k in range(7):
        first[2 * k].wait_send()
        first[2 * k + 1].wait()
    for k in order:
        to_y[k].wait_send()
        to_core[k].wait()
        to_core[8 + k].wait()


def product_kernel(cap, meta_ref, tiles_ref, green_ref, total_ref):
    part = cap // 4
    side = tiles_ref.shape[-1]
    total_ref[...] = jnp.zeros_like(total_ref)

    def add_all(flipped):
        @pl.loop(0, tiles_ref.shape[0] * tiles_ref.shape[1] // 2)
        def _(i):
            terms = []
            for h in range(2):
                n = 2 * i + h
                quarter, source = n // tiles_ref.shape[1], n % tiles_ref.shape[1]
                for j in range(part):
                    code = meta_ref[source, 0, quarter * part + j]
                    start = pl.multiple_of((code % 256) * side, side)
                    pair = (tiles_ref[quarter, source, j], green_ref[:, pl.ds(start, side)])
                    terms.append((code // 256, lax.dot_general(
                        *(pair[::-1] if flipped else pair), (((1,), (1,)), ((), ())),
                        preferred_element_type=jnp.float32)))
            for aux, term in terms:
                total_ref[aux] += term

    core = lax.axis_index("row") % 2
    pl.when(core == 0)(lambda: add_all(False))
    pl.when(core == 1)(lambda: add_all(True))


def pair_kernel(total_ref, chi_ref, right_in, left_in, done, occ_in, virt_in, plane_in, line_in,
                right_send, right_recv, left_send, left_recv, occ_send, occ_recv, virt_send, virt_recv,
                plane_send, plane_recv, line_send, line_recv):
    y, core, x, z = place()
    row = 2 * y + core
    count = total_ref.shape[0]
    rows = right_in.shape[1]
    thin = rows // 2
    steps = STEPS
    size = count // steps
    diagonal = x == y
    end = jnp.logical_or(z == 0, z == 3)

    def device(number):
        return (2 * (number // 4) + number % 2, (number // 2) % 2, z)

    mine = 4 * y + 2 * x + core
    barrier = pltpu.get_barrier_semaphore()
    for k in range(1, 4):
        pl.semaphore_signal(barrier, inc=1, device_id=(row, x, (z + k) % 4), device_id_type=MESH)
    for k in range(1, 8):
        pl.semaphore_signal(barrier, inc=1, device_id=device((mine + k) % 8), device_id_type=MESH)
    pl.semaphore_wait(barrier, 10)

    def chunk(c):
        return pl.ds(c * size, size)

    def right(c, source):
        return pltpu.make_async_remote_copy(
            src_ref=source, dst_ref=right_in.at[chunk(c)], send_sem=right_send.at[c], recv_sem=right_recv.at[c],
            device_id=(row, x, (z + 1) % 4), device_id_type=MESH)

    def left(c, source):
        return pltpu.make_async_remote_copy(
            src_ref=source, dst_ref=left_in.at[chunk(c)], send_sem=left_send.at[c], recv_sem=left_recv.at[c],
            device_id=(row, x, (z + 3) % 4), device_id_type=MESH)

    def pass_right(c):
        right(c, right_in.at[chunk(c)]).wait_recv()
        right_in[chunk(c)] += total_ref[chunk(c), rows:]
        right(c, right_in.at[chunk(c)]).start()

    def pass_left(c):
        left(c, left_in.at[chunk(c)]).wait_recv()
        left_in[chunk(c)] += total_ref[chunk(c), :rows]
        left(c, left_in.at[chunk(c)]).start()

    def occ_copy(c):
        return pltpu.make_async_remote_copy(
            src_ref=done.at[chunk(c), thin:], dst_ref=occ_in.at[chunk(c)], send_sem=occ_send.at[c],
            recv_sem=occ_recv.at[c], device_id=(2 * y + 1 - core, x, z), device_id_type=MESH)

    def virt_copy(c, kk):
        return pltpu.make_async_remote_copy(
            src_ref=done.at[chunk(c), kk * thin:(kk + 1) * thin], dst_ref=virt_in.at[chunk(c)],
            send_sem=virt_send.at[c, kk], recv_sem=virt_recv.at[c], device_id=(2 * x + kk, y, z),
            device_id_type=MESH)

    def hand_out(c):
        @pl.when(core == 0)
        def _():
            occ_copy(c).start()
            occ_in[chunk(c)] = done[chunk(c), :thin]

        @pl.when(core == 1)
        def _():
            virt_copy(c, 0).start()

            @pl.when(diagonal)
            def _():
                virt_in[chunk(c)] = done[chunk(c), thin:]

            @pl.when(jnp.logical_not(diagonal))
            def _():
                virt_copy(c, 1).start()

    lag = 2

    @pl.when(z == 0)
    def _():
        for c in range(steps + lag):
            if c < steps:
                if c >= 3:
                    right(c - 3, total_ref.at[chunk(c - 3), rows:]).wait_send()
                right(c, total_ref.at[chunk(c), rows:]).start()
            if c >= lag:
                e = c - lag
                left(e, left_in.at[chunk(e)]).wait_recv()
                done[chunk(e)] = left_in[chunk(e)] + total_ref[chunk(e), :rows]
                hand_out(e)
        for c in range(steps - 3, steps):
            right(c, total_ref.at[chunk(c), rows:]).wait_send()

    @pl.when(z == 3)
    def _():
        for c in range(steps + lag):
            if c < steps:
                if c >= 3:
                    left(c - 3, total_ref.at[chunk(c - 3), :rows]).wait_send()
                left(c, total_ref.at[chunk(c), :rows]).start()
            if c >= lag:
                e = c - lag
                right(e, right_in.at[chunk(e)]).wait_recv()
                done[chunk(e)] = right_in[chunk(e)] + total_ref[chunk(e), rows:]
                hand_out(e)
        for c in range(steps - 3, steps):
            left(c, total_ref.at[chunk(c), :rows]).wait_send()

    def relay(near, far):
        for c in range(steps + 1):
            if c < steps:
                near(c)
            if c >= 1:
                far(c - 1)

    pl.when(z == 1)(lambda: relay(pass_right, pass_left))
    pl.when(z == 2)(lambda: relay(pass_left, pass_right))

    @pl.when(jnp.logical_not(end))
    def _():
        for c in range(steps):
            right(c, right_in.at[chunk(c)]).wait_send()
            left(c, left_in.at[chunk(c)]).wait_send()

    def plane(k):
        return pltpu.make_async_remote_copy(
            src_ref=plane_in.at[mine], dst_ref=plane_in.at[mine], send_sem=plane_send.at[k],
            recv_sem=plane_recv.at[k], device_id=device((mine + k) % 8), device_id_type=MESH)

    def line(which, k):
        return pltpu.make_async_remote_copy(
            src_ref=line_in.at[which], dst_ref=line_in.at[which], send_sem=line_send.at[k],
            recv_sem=line_recv.at[which], device_id=(row, x, (z + k) % 4), device_id_type=MESH)

    @pl.when(end)
    def _():
        for c in range(steps):
            @pl.when(core == 1)
            def _():
                occ_copy(c).wait_recv()

            @pl.when(jnp.logical_not(jnp.logical_and(diagonal, core == 1)))
            def _():
                virt_copy(c, 0).wait_recv()
        chi = jnp.zeros((count, count), jnp.float32)
        for i in range(0, thin, 2):
            first = jnp.concatenate([occ_in[:, i, :], occ_in[:, i + 1, :]], axis=1)
            second = jnp.concatenate([virt_in[:, i, :], virt_in[:, i + 1, :]], axis=1)
            chi += lax.dot_general(first, second, (((1,), (1,)), ((), ())), precision=lax.Precision.HIGHEST,
                                   preferred_element_type=jnp.float32)
        plane_in[mine] = jnp.pad(chi, ((0, 0), (0, 128 - count)))
        for k in range(1, 8):
            plane(k).start()
        for k in range(1, 8):
            plane(k).wait_recv()
        summed = plane_in[0]
        for k in range(1, 8):
            summed += plane_in[k]

        @pl.when(z == 0)
        def _():
            line_in[0] = summed
            for k in (3, 2, 1):
                line(0, k).start()

        @pl.when(z == 3)
        def _():
            line_in[1] = summed
            for k in (1, 2, 3):
                line(1, k).start()

    @pl.when(z > 0)
    def _():
        line(0, 1).wait_recv()

    @pl.when(z < 3)
    def _():
        line(1, 1).wait_recv()

    chi_ref[...] = (line_in[0] + line_in[1])[:, :count]

    @pl.when(end)
    def _():
        for k in range(1, 8):
            plane(k).wait_send()
        for k in range(1, 4):
            line(0, k).wait_send()
        for c in range(steps):
            @pl.when(core == 0)
            def _():
                occ_copy(c).wait_send()

            @pl.when(core == 1)
            def _():
                virt_copy(c, 0).wait_send()

                @pl.when(jnp.logical_not(diagonal))
                def _():
                    virt_copy(c, 1).wait_send()


def on_slice(blocks, block_aux, block_row, block_col, extents, occ_green, virt_green):
    held, side, _ = blocks.shape
    layers, owners = 4, 8
    cap = held // owners + 1
    depth, width = occ_green.shape
    smem, vmem = pl.BlockSpec(memory_space=pltpu.SMEM), pl.BlockSpec(memory_space=pltpu.VMEM)
    f32, i32 = jnp.float32, jnp.int32
    dma = pltpu.SemaphoreType.DMA

    def bind(kernel, *sizes):
        def run(*refs):
            kernel(*sizes, *refs)
        return run

    pick, meta = pl.pallas_call(
        bind(slot_kernel, cap, layers, depth // side),
        out_shape=(jax.ShapeDtypeStruct((128,), i32), jax.ShapeDtypeStruct((owners, 8, 128), i32)),
        in_specs=[smem] * 4,
        out_specs=(smem, smem),
        name="slots",
    )(block_aux, block_row, block_col, extents)
    part = cap // 4
    tiles, meta, green = pl.pallas_call(
        bind(exchange_kernel, cap),
        out_shape=(
            jax.ShapeDtypeStruct((4, owners, part, side, side), blocks.dtype),
            jax.ShapeDtypeStruct((owners, 8, 128), i32),
            jax.ShapeDtypeStruct((2 * width, depth), occ_green.dtype),
        ),
        in_specs=[smem, vmem, vmem, vmem, vmem],
        out_specs=(vmem, vmem, vmem),
        scratch_shapes=[
            pltpu.VMEM((7, part, side, side), blocks.dtype),
            dma((7,)), dma((7,)), dma((7,)), dma((7,)), dma((8,)), dma((8,)), dma((16,)), dma((16,)),
            dma(()), dma(()),
        ],
        compiler_params=pltpu.CompilerParams(collective_id=0, has_side_effects=True, vmem_limit_bytes=VMEM_LIMIT),
        name="exchange",
    )(pick, meta, blocks, occ_green.T, virt_green.T)
    total = pl.pallas_call(
        bind(product_kernel, cap),
        out_shape=jax.ShapeDtypeStruct((NP, side, 2 * width), f32),
        in_specs=[smem, vmem, vmem],
        out_specs=vmem,
        compiler_params=pltpu.CompilerParams(vmem_limit_bytes=VMEM_LIMIT),
        name="product",
    )(meta, tiles, green)
    rows, part_rows = side // 2, side // 4
    return pl.pallas_call(
        pair_kernel,
        out_shape=jax.ShapeDtypeStruct((NP, NP), f32),
        in_specs=[vmem],
        out_specs=vmem,
        scratch_shapes=[
            pltpu.VMEM((NP, rows, side), f32),
            pltpu.VMEM((NP, rows, side), f32),
            pltpu.VMEM((NP, rows, side), f32),
            pltpu.VMEM((NP, part_rows, side), f32),
            pltpu.VMEM((NP, part_rows, side), f32),
            pltpu.VMEM((8, NP, 128), f32),
            pltpu.VMEM((2, NP, 128), f32),
            dma((STEPS,)), dma((STEPS,)), dma((STEPS,)), dma((STEPS,)), dma((STEPS,)), dma((STEPS,)),
            dma((STEPS, 2)), dma((STEPS,)), dma((8,)), dma((8,)), dma((4,)), dma((2,)),
        ],
        compiler_params=pltpu.CompilerParams(collective_id=1, has_side_effects=True, vmem_limit_bytes=VMEM_LIMIT),
        name="pair",
    )(total)


def on_device(blocks, block_aux, block_row, block_col, extents, occ_green, virt_green):
    row_count = lax.axis_size("row")
    col_count = lax.axis_size("col")
    layer_count = lax.axis_size("layer")
    held_count = blocks.shape[0]
    tile_side = blocks.shape[1]
    aux_count = NP
    owner_count = col_count * layer_count
    capacity = max(2, held_count // owner_count + 1)
    layer_blocks = occ_green.shape[0] // tile_side
    columns = jnp.arange(tile_side, dtype=jnp.int32)
    masked_tiles = jnp.where(
        columns[None, None, :] < extents[:, None, None], blocks, jnp.zeros((), blocks.dtype)
    )
    layer_of = block_col // layer_blocks
    target = block_row * layer_count + layer_of
    kept_col = block_col - layer_of * layer_blocks
    marked = (target[:, None] == jnp.arange(owner_count, dtype=jnp.int32)[None, :]).astype(
        jnp.int32
    )
    earlier = jnp.cumsum(marked, axis=0) - marked
    placed = target * capacity + jnp.sum(earlier * marked, axis=1)
    send_tiles = (
        jnp.zeros((owner_count * capacity, tile_side, tile_side), blocks.dtype)
        .at[placed]
        .set(masked_tiles)
    )
    send_meta = (
        jnp.zeros((owner_count * capacity, 2), jnp.int32)
        .at[placed]
        .set(jnp.stack([block_aux, kept_col], axis=1))
    )
    send_tiles = send_tiles.reshape(col_count, layer_count, capacity, tile_side, tile_side)
    send_meta = send_meta.reshape(col_count, layer_count, capacity, 2)
    total_slots = col_count * layer_count * capacity
    got_tiles, got_meta = (
        lax.all_to_all(
            send_tiles.reshape(total_slots, tile_side, tile_side),
            ("col", "layer"),
            split_axis=0,
            concat_axis=0,
            tiled=True,
        ),
        lax.all_to_all(
            send_meta.reshape(total_slots, 2),
            ("col", "layer"),
            split_axis=0,
            concat_axis=0,
            tiled=True,
        ),
    )
    group_size = col_count * capacity
    got_tiles = got_tiles.reshape(layer_count, group_size, tile_side, tile_side)
    got_meta = got_meta.reshape(layer_count, group_size, 2)
    occ_cols, virt_cols = (occ_green, virt_green)
    width_here = occ_cols.shape[1]
    offsets = jnp.arange(tile_side, dtype=jnp.int32)

    def add_group(totals, record):
        occ_total, virt_total = totals
        tile_group, meta_group = record
        row_index = meta_group[:, 1][:, None] * tile_side + offsets[None, :]
        occ_rows = occ_cols[row_index]
        virt_rows = virt_cols[row_index]
        occ_term = jnp.einsum(
            "gsv,gls->gvl", occ_rows, tile_group, preferred_element_type=jnp.float32
        )
        virt_term = jnp.einsum(
            "gvs,gsl->gvl", tile_group, virt_rows, preferred_element_type=jnp.float32
        )
        aux_index = meta_group[:, 0]
        return (
            (occ_total.at[aux_index].add(occ_term), virt_total.at[aux_index].add(virt_term)),
            None,
        )

    start_totals = (
        jnp.zeros((aux_count, width_here, tile_side), jnp.float32),
        jnp.zeros((aux_count, tile_side, width_here), jnp.float32),
    )
    (occ_total, virt_total), _ = lax.scan(add_group, start_totals, (got_tiles, got_meta))
    occ_done, virt_done = (
        lax.psum_scatter(occ_total, "layer", scatter_dimension=1, tiled=True),
        lax.psum_scatter(virt_total, "layer", scatter_dimension=2, tiled=True),
    )
    mesh_count = row_count * layer_count
    thin_rows = tile_side // mesh_count
    stack_count = mesh_count // col_count
    narrow = occ_done.shape[1]
    occ_five = occ_done.reshape(aux_count, 1, col_count, thin_rows, tile_side)
    virt_five = virt_done.reshape(aux_count, stack_count, col_count, thin_rows, narrow)
    occ_moved, virt_moved = (
        lax.all_to_all(occ_five, "col", split_axis=2, concat_axis=1, tiled=True),
        lax.all_to_all(virt_five, "col", split_axis=2, concat_axis=1, tiled=True),
    )
    virt_four = virt_moved.reshape(aux_count, mesh_count, thin_rows, narrow)
    virt_back = lax.all_to_all(virt_four, ("row", "layer"), split_axis=1, concat_axis=3, tiled=True)
    occ_final = occ_moved.reshape(aux_count, col_count, thin_rows, tile_side)
    virt_final = virt_back.reshape(aux_count, thin_rows, col_count, tile_side)
    chi_part = jnp.einsum(
        "pcji,qjci->pq",
        occ_final,
        virt_final,
        precision=lax.Precision.HIGHEST,
        preferred_element_type=jnp.float32,
    )
    return lax.psum(chi_part, ("row", "col", "layer"))


def solution(mesh):
    in_specs = (
        P(("col", "layer"), None, None),
        P(("col", "layer")),
        P(("col", "layer")),
        P(("col", "layer")),
        P(("col", "layer")),
        P("layer", "row"),
        P("layer", "row"),
    )
    out_specs = P()
    side_of = (mesh.shape["row"], mesh.shape["col"], mesh.shape["layer"])
    return jax.shard_map(
        on_slice if side_of == (4, 2, 4) else on_device, mesh=mesh, in_specs=in_specs, out_specs=out_specs, check_vma=False
    )
```

```python
import jax
import jax.numpy as jnp
from jax import lax
from jax.experimental import pallas as pl
from jax.experimental.pallas import tpu as pltpu
from jax.sharding import PartitionSpec as P

NP = 24
MESH = pl.DeviceIdType.MESH
VMEM_LIMIT = 40 * 1024 * 1024
STEPS = 8
OFFSETS = ((0, 3), (1, 0), (1, 2), (0, 1), (1, 3), (0, 2), (1, 1))


def slot_kernel(cap, layers, layer_blocks, aux_ref, row_ref, col_ref, ext_ref, code_ref):
    held = aux_ref.shape[0]
    owners = code_ref.shape[1]
    for o in range(owners):
        for j in range(cap):
            code_ref[0, o, 0, j] = 0
            code_ref[1, o, 0, j] = 0

    def put(n, counts):
        block = col_ref[n]
        layer = jnp.int32(0)
        for edge in range(1, layers):
            layer += (block >= edge * layer_blocks).astype(jnp.int32)
        owner = row_ref[n] * layers + layer
        rank = lax.shift_right_logical(counts, 4 * owner) & 15
        code_ref[0, owner, 0, rank] = n * 256 + ext_ref[n]
        code_ref[1, owner, 0, rank] = aux_ref[n] * 256 + block - layer * layer_blocks
        return counts + lax.shift_left(jnp.int32(1), 4 * owner)

    lax.fori_loop(0, held, put, jnp.int32(0), unroll=8)


def place():
    row, col, layer = lax.axis_index("row"), lax.axis_index("col"), lax.axis_index("layer")
    return row // 2, row % 2, col, layer


def exchange_kernel(cap, code_ref, blocks_hbm, occ_hbm, virt_hbm, tiles_ref, meta_out, green_ref,
                    blocks_ref, own_green, codes, meta_ref, send_buf, load_sem, meta_send, meta_recv, tile_send, tile_recv,
                    y_send, y_recv, core_send, core_recv, green_send, green_recv):
    y, core, col, layer = place()
    row = 2 * y + core
    across = 2 * (1 - y) + core
    sibling = 2 * y + 1 - core
    me = col * 4 + layer
    part = cap // 4
    side = blocks_ref.shape[1]
    half = own_green.shape[0]
    own_rows = pl.ds(pl.multiple_of(core * half, half), half)

    load_codes = pltpu.make_async_copy(code_ref.at[0], codes, load_sem.at[0])
    load_meta = pltpu.make_async_copy(code_ref.at[1], meta_ref, load_sem.at[1])
    load_blocks = pltpu.make_async_copy(blocks_hbm, blocks_ref, load_sem.at[2])
    load_codes.start()
    load_meta.start()
    load_blocks.start()

    def load_own(source):
        return pltpu.make_async_copy(source, green_ref.at[own_rows], load_sem.at[3])

    def load_other(source):
        return pltpu.make_async_copy(source, own_green, load_sem.at[4])

    @pl.when(core == 0)
    def _():
        load_other(virt_hbm).start()
        load_own(occ_hbm).start()

    @pl.when(core == 1)
    def _():
        load_other(occ_hbm).start()
        load_own(virt_hbm).start()

    layers_by = (layer, layer + 1 - 2 * (layer % 2), (layer + 2) % 4, 3 - layer)
    barrier = pltpu.get_barrier_semaphore()
    peers = [(row, 1 - col if dc else col, layers_by[dl]) for dc, dl in OFFSETS]
    for peer in peers + [(across, col, layer), (sibling, col, layer)]:
        pl.semaphore_signal(barrier, inc=1, device_id=peer, device_id_type=MESH)
    pl.semaphore_wait(barrier, len(peers) + 2)

    greens = pltpu.make_async_remote_copy(
        src_ref=own_green, dst_ref=green_ref.at[own_rows], send_sem=green_send, recv_sem=green_recv,
        device_id=(sibling, col, layer), device_id_type=MESH)
    lanes = lax.broadcasted_iota(jnp.int32, (side, side), 1)

    def packed(owner, j):
        pick = codes[owner, 0, row * part + j]
        tile = blocks_ref[pick // 256]
        return jnp.where(lanes < pick % 256, tile.astype(jnp.float32), 0.0).astype(tile.dtype)

    def owner_of(peer):
        return peer[1] * 4 + peer[2]

    def pack(k):
        for j in range(part):
            send_buf[k, j] = packed(owner_of(peers[k]), j)

    tile_copies = [pltpu.make_async_remote_copy(
        src_ref=send_buf.at[k], dst_ref=tiles_ref.at[row, me], send_sem=tile_send.at[k],
        recv_sem=tile_recv.at[k], device_id=peer, device_id_type=MESH) for k, peer in enumerate(peers)]
    meta_copies = [pltpu.make_async_remote_copy(
        src_ref=meta_ref.at[owner_of(peer)], dst_ref=meta_out.at[me], send_sem=meta_send.at[k],
        recv_sem=meta_recv.at[k], device_id=peer, device_id_type=MESH) for k, peer in enumerate(peers)]

    def forward(quarter, source, send, recv, k, target):
        copy = pltpu.make_async_remote_copy(
            src_ref=tiles_ref.at[quarter, source], dst_ref=tiles_ref.at[quarter, source],
            send_sem=send.at[k], recv_sem=recv.at[k], device_id=(target, col, layer), device_id_type=MESH)
        copy.start()
        return copy

    sources = [owner_of(peer) for peer in peers] + [me]
    order = [7] + list(range(7))
    to_y, to_core = {}, {}
    window = 3
    load_codes.wait()
    load_blocks.wait()

    def send(k):
        pack(k)
        tile_copies[k].start()

    send(0)
    for j in range(part):
        tiles_ref[row, me, j] = packed(me, j)
    to_y[7] = forward(row, me, y_send, y_recv, 7, across)
    to_core[7] = forward(row, me, core_send, core_recv, 7, sibling)
    for k in range(1, window):
        send(k)
    load_other(virt_hbm).wait()
    greens.start()
    load_meta.wait()
    for copy in meta_copies:
        copy.start()
    meta_out[me] = meta_ref[me]

    for k in range(window, 7):
        pack(k)
    for k in range(7):
        if k + window < 7:
            tile_copies[k].wait_send()
            tile_copies[k + window].start()
        tile_copies[k].wait_recv()
        to_y[k] = forward(row, sources[k], y_send, y_recv, k, across)
        to_core[k] = forward(row, sources[k], core_send, core_recv, k, sibling)
        if k >= 1:
            e = order[k - 1]
            to_y[e].wait_recv()
            to_core[8 + e] = forward(across, sources[e], core_send, core_recv, 8 + e, sibling)

    for e in order[6:]:
        to_y[e].wait_recv()
        to_core[8 + e] = forward(across, sources[e], core_send, core_recv, 8 + e, sibling)
    load_own(occ_hbm).wait()
    greens.wait()
    for k in range(7):
        if k + window >= 7:
            tile_copies[k].wait_send()
        meta_copies[k].wait()
    for k in order:
        to_y[k].wait_send()
        to_core[k].wait()
        to_core[8 + k].wait()


def product_kernel(cap, meta_ref, tiles_ref, green_ref, total_ref):
    part = cap // 4
    side = tiles_ref.shape[-1]
    total_ref[...] = jnp.zeros_like(total_ref)

    def add_all(flipped):
        @pl.loop(0, tiles_ref.shape[0] * tiles_ref.shape[1] // 2)
        def _(i):
            terms = []
            for h in range(2):
                n = 2 * i + h
                quarter, source = n // tiles_ref.shape[1], n % tiles_ref.shape[1]
                for j in range(part):
                    code = meta_ref[source, 0, quarter * part + j]
                    start = pl.multiple_of((code % 256) * side, side)
                    pair = (tiles_ref[quarter, source, j], green_ref[:, pl.ds(start, side)])
                    terms.append((code // 256, lax.dot_general(
                        *(pair[::-1] if flipped else pair), (((1,), (1,)), ((), ())),
                        preferred_element_type=jnp.float32)))
            for aux, term in terms:
                total_ref[aux] += term

    core = lax.axis_index("row") % 2
    pl.when(core == 0)(lambda: add_all(False))
    pl.when(core == 1)(lambda: add_all(True))


def pair_kernel(total_ref, chi_ref, right_in, left_in, done, occ_in, virt_in, plane_in, line_in,
                right_send, right_recv, left_send, left_recv, occ_send, occ_recv, virt_send, virt_recv,
                plane_send, plane_recv, line_send, line_recv):
    y, core, x, z = place()
    row = 2 * y + core
    count = total_ref.shape[0]
    rows = right_in.shape[1]
    thin = rows // 2
    steps = STEPS
    size = count // steps
    diagonal = x == y
    end = jnp.logical_or(z == 0, z == 3)

    def device(number):
        return (2 * (number // 4) + number % 2, (number // 2) % 2, z)

    mine = 4 * y + 2 * x + core
    barrier = pltpu.get_barrier_semaphore()
    for k in range(1, 4):
        pl.semaphore_signal(barrier, inc=1, device_id=(row, x, (z + k) % 4), device_id_type=MESH)
    for k in range(1, 8):
        pl.semaphore_signal(barrier, inc=1, device_id=device((mine + k) % 8), device_id_type=MESH)
    pl.semaphore_wait(barrier, 10)

    def chunk(c):
        return pl.ds(c * size, size)

    def right(c, source):
        return pltpu.make_async_remote_copy(
            src_ref=source, dst_ref=right_in.at[chunk(c)], send_sem=right_send.at[c], recv_sem=right_recv.at[c],
            device_id=(row, x, (z + 1) % 4), device_id_type=MESH)

    def left(c, source):
        return pltpu.make_async_remote_copy(
            src_ref=source, dst_ref=left_in.at[chunk(c)], send_sem=left_send.at[c], recv_sem=left_recv.at[c],
            device_id=(row, x, (z + 3) % 4), device_id_type=MESH)

    def pass_right(c):
        right(c, right_in.at[chunk(c)]).wait_recv()
        right_in[chunk(c)] += total_ref[chunk(c), rows:]
        right(c, right_in.at[chunk(c)]).start()

    def pass_left(c):
        left(c, left_in.at[chunk(c)]).wait_recv()
        left_in[chunk(c)] += total_ref[chunk(c), :rows]
        left(c, left_in.at[chunk(c)]).start()

    def occ_copy(c):
        return pltpu.make_async_remote_copy(
            src_ref=done.at[chunk(c), thin:], dst_ref=occ_in.at[chunk(c)], send_sem=occ_send.at[c],
            recv_sem=occ_recv.at[c], device_id=(2 * y + 1 - core, x, z), device_id_type=MESH)

    def virt_copy(c, kk):
        return pltpu.make_async_remote_copy(
            src_ref=done.at[chunk(c), kk * thin:(kk + 1) * thin], dst_ref=virt_in.at[chunk(c)],
            send_sem=virt_send.at[c, kk], recv_sem=virt_recv.at[c], device_id=(2 * x + kk, y, z),
            device_id_type=MESH)

    def hand_out(c):
        @pl.when(core == 0)
        def _():
            occ_copy(c).start()
            occ_in[chunk(c)] = done[chunk(c), :thin]

        @pl.when(core == 1)
        def _():
            virt_copy(c, 0).start()

            @pl.when(diagonal)
            def _():
                virt_in[chunk(c)] = done[chunk(c), thin:]

            @pl.when(jnp.logical_not(diagonal))
            def _():
                virt_copy(c, 1).start()

    lag = 6

    @pl.when(z == 0)
    def _():
        for c in range(steps + lag):
            if c < steps:
                if c >= 3:
                    right(c - 3, total_ref.at[chunk(c - 3), rows:]).wait_send()
                right(c, total_ref.at[chunk(c), rows:]).start()
            if c >= lag:
                e = c - lag
                left(e, left_in.at[chunk(e)]).wait_recv()
                done[chunk(e)] = left_in[chunk(e)] + total_ref[chunk(e), :rows]
                hand_out(e)
        for c in range(steps - 3, steps):
            right(c, total_ref.at[chunk(c), rows:]).wait_send()

    @pl.when(z == 3)
    def _():
        for c in range(steps + lag):
            if c < steps:
                if c >= 3:
                    left(c - 3, total_ref.at[chunk(c - 3), :rows]).wait_send()
                left(c, total_ref.at[chunk(c), :rows]).start()
            if c >= lag:
                e = c - lag
                right(e, right_in.at[chunk(e)]).wait_recv()
                done[chunk(e)] = right_in[chunk(e)] + total_ref[chunk(e), rows:]
                hand_out(e)
        for c in range(steps - 3, steps):
            left(c, total_ref.at[chunk(c), :rows]).wait_send()

    def relay(near, far):
        for c in range(steps + 2):
            if c < steps:
                near(c)
            if c >= 2:
                far(c - 2)

    pl.when(z == 1)(lambda: relay(pass_right, pass_left))
    pl.when(z == 2)(lambda: relay(pass_left, pass_right))

    @pl.when(jnp.logical_not(end))
    def _():
        for c in range(steps):
            right(c, right_in.at[chunk(c)]).wait_send()
            left(c, left_in.at[chunk(c)]).wait_send()

    def plane(k):
        return pltpu.make_async_remote_copy(
            src_ref=plane_in.at[mine], dst_ref=plane_in.at[mine], send_sem=plane_send.at[k],
            recv_sem=plane_recv.at[k], device_id=device((mine + k) % 8), device_id_type=MESH)

    def line(which, k):
        return pltpu.make_async_remote_copy(
            src_ref=line_in.at[which], dst_ref=line_in.at[which], send_sem=line_send.at[k],
            recv_sem=line_recv.at[which], device_id=(row, x, (z + k) % 4), device_id_type=MESH)

    @pl.when(end)
    def _():
        for c in range(steps):
            @pl.when(core == 1)
            def _():
                occ_copy(c).wait_recv()

            @pl.when(jnp.logical_not(jnp.logical_and(diagonal, core == 1)))
            def _():
                virt_copy(c, 0).wait_recv()
        chi = jnp.zeros((count, count), jnp.float32)
        for i in range(0, thin, 2):
            first = jnp.concatenate([occ_in[:, i, :], occ_in[:, i + 1, :]], axis=1)
            second = jnp.concatenate([virt_in[:, i, :], virt_in[:, i + 1, :]], axis=1)
            chi += lax.dot_general(first, second, (((1,), (1,)), ((), ())), precision=lax.Precision.HIGHEST,
                                   preferred_element_type=jnp.float32)
        plane_in[mine] = jnp.pad(chi, ((0, 0), (0, 128 - count)))
        for k in range(1, 8):
            plane(k).start()
        for k in range(1, 8):
            plane(k).wait_recv()
        summed = plane_in[0]
        for k in range(1, 8):
            summed += plane_in[k]

        @pl.when(z == 0)
        def _():
            line_in[0] = summed
            for k in (3, 2, 1):
                line(0, k).start()

        @pl.when(z == 3)
        def _():
            line_in[1] = summed
            for k in (1, 2, 3):
                line(1, k).start()

    @pl.when(z > 0)
    def _():
        line(0, 1).wait_recv()

    @pl.when(z < 3)
    def _():
        line(1, 1).wait_recv()

    chi_ref[...] = (line_in[0] + line_in[1])[:, :count]

    @pl.when(end)
    def _():
        for k in range(1, 8):
            plane(k).wait_send()
        for k in range(1, 4):
            line(0, k).wait_send()
        for c in range(steps):
            @pl.when(core == 0)
            def _():
                occ_copy(c).wait_send()

            @pl.when(core == 1)
            def _():
                virt_copy(c, 0).wait_send()

                @pl.when(jnp.logical_not(diagonal))
                def _():
                    virt_copy(c, 1).wait_send()


def on_slice(blocks, block_aux, block_row, block_col, extents, occ_green, virt_green):
    held, side, _ = blocks.shape
    layers, owners = 4, 8
    cap = held // owners + 1
    depth, width = occ_green.shape
    smem, vmem = pl.BlockSpec(memory_space=pltpu.SMEM), pl.BlockSpec(memory_space=pltpu.VMEM)
    f32, i32 = jnp.float32, jnp.int32
    dma = pltpu.SemaphoreType.DMA

    def bind(kernel, *sizes):
        def run(*refs):
            kernel(*sizes, *refs)
        return run

    codes = pl.pallas_call(
        bind(slot_kernel, cap, layers, depth // side),
        out_shape=jax.ShapeDtypeStruct((2, owners, 8, 128), i32),
        in_specs=[smem] * 4,
        out_specs=smem,
        name="slots",
    )(block_aux, block_row, block_col, extents)
    part = cap // 4
    tiles, meta, green = pl.pallas_call(
        bind(exchange_kernel, cap),
        out_shape=(
            jax.ShapeDtypeStruct((4, owners, part, side, side), blocks.dtype),
            jax.ShapeDtypeStruct((owners, 8, 128), i32),
            jax.ShapeDtypeStruct((2 * width, depth), occ_green.dtype),
        ),
        in_specs=[pl.BlockSpec(memory_space=pl.ANY)] * 4,
        out_specs=(vmem, vmem, vmem),
        scratch_shapes=[
            pltpu.VMEM(blocks.shape, blocks.dtype),
            pltpu.VMEM((width, depth), occ_green.dtype),
            pltpu.SMEM((owners, 8, 128), i32),
            pltpu.VMEM((owners, 8, 128), i32),
            pltpu.VMEM((7, part, side, side), blocks.dtype),
            dma((5,)),
            dma((7,)), dma((7,)), dma((7,)), dma((7,)), dma((8,)), dma((8,)), dma((16,)), dma((16,)),
            dma(()), dma(()),
        ],
        compiler_params=pltpu.CompilerParams(collective_id=0, has_side_effects=True, vmem_limit_bytes=VMEM_LIMIT),
        name="exchange",
    )(codes, blocks, occ_green.T, virt_green.T)
    total = pl.pallas_call(
        bind(product_kernel, cap),
        out_shape=jax.ShapeDtypeStruct((NP, side, 2 * width), f32),
        in_specs=[smem, vmem, vmem],
        out_specs=vmem,
        compiler_params=pltpu.CompilerParams(vmem_limit_bytes=VMEM_LIMIT),
        name="product",
    )(meta, tiles, green)
    rows, part_rows = side // 2, side // 4
    return pl.pallas_call(
        pair_kernel,
        out_shape=jax.ShapeDtypeStruct((NP, NP), f32),
        in_specs=[vmem],
        out_specs=vmem,
        scratch_shapes=[
            pltpu.VMEM((NP, rows, side), f32),
            pltpu.VMEM((NP, rows, side), f32),
            pltpu.VMEM((NP, rows, side), f32),
            pltpu.VMEM((NP, part_rows, side), f32),
            pltpu.VMEM((NP, part_rows, side), f32),
            pltpu.VMEM((8, NP, 128), f32),
            pltpu.VMEM((2, NP, 128), f32),
            dma((STEPS,)), dma((STEPS,)), dma((STEPS,)), dma((STEPS,)), dma((STEPS,)), dma((STEPS,)),
            dma((STEPS, 2)), dma((STEPS,)), dma((8,)), dma((8,)), dma((4,)), dma((2,)),
        ],
        compiler_params=pltpu.CompilerParams(collective_id=1, has_side_effects=True, vmem_limit_bytes=VMEM_LIMIT),
        name="pair",
    )(total)


def on_device(blocks, block_aux, block_row, block_col, extents, occ_green, virt_green):
    row_count = lax.axis_size("row")
    col_count = lax.axis_size("col")
    layer_count = lax.axis_size("layer")
    held_count = blocks.shape[0]
    tile_side = blocks.shape[1]
    aux_count = NP
    owner_count = col_count * layer_count
    capacity = max(2, held_count // owner_count + 1)
    layer_blocks = occ_green.shape[0] // tile_side
    columns = jnp.arange(tile_side, dtype=jnp.int32)
    masked_tiles = jnp.where(
        columns[None, None, :] < extents[:, None, None], blocks, jnp.zeros((), blocks.dtype)
    )
    layer_of = block_col // layer_blocks
    target = block_row * layer_count + layer_of
    kept_col = block_col - layer_of * layer_blocks
    marked = (target[:, None] == jnp.arange(owner_count, dtype=jnp.int32)[None, :]).astype(
        jnp.int32
    )
    earlier = jnp.cumsum(marked, axis=0) - marked
    placed = target * capacity + jnp.sum(earlier * marked, axis=1)
    send_tiles = (
        jnp.zeros((owner_count * capacity, tile_side, tile_side), blocks.dtype)
        .at[placed]
        .set(masked_tiles)
    )
    send_meta = (
        jnp.zeros((owner_count * capacity, 2), jnp.int32)
        .at[placed]
        .set(jnp.stack([block_aux, kept_col], axis=1))
    )
    send_tiles = send_tiles.reshape(col_count, layer_count, capacity, tile_side, tile_side)
    send_meta = send_meta.reshape(col_count, layer_count, capacity, 2)
    total_slots = col_count * layer_count * capacity
    got_tiles, got_meta = (
        lax.all_to_all(
            send_tiles.reshape(total_slots, tile_side, tile_side),
            ("col", "layer"),
            split_axis=0,
            concat_axis=0,
            tiled=True,
        ),
        lax.all_to_all(
            send_meta.reshape(total_slots, 2),
            ("col", "layer"),
            split_axis=0,
            concat_axis=0,
            tiled=True,
        ),
    )
    group_size = col_count * capacity
    got_tiles = got_tiles.reshape(layer_count, group_size, tile_side, tile_side)
    got_meta = got_meta.reshape(layer_count, group_size, 2)
    occ_cols, virt_cols = (occ_green, virt_green)
    width_here = occ_cols.shape[1]
    offsets = jnp.arange(tile_side, dtype=jnp.int32)

    def add_group(totals, record):
        occ_total, virt_total = totals
        tile_group, meta_group = record
        row_index = meta_group[:, 1][:, None] * tile_side + offsets[None, :]
        occ_rows = occ_cols[row_index]
        virt_rows = virt_cols[row_index]
        occ_term = jnp.einsum(
            "gsv,gls->gvl", occ_rows, tile_group, preferred_element_type=jnp.float32
        )
        virt_term = jnp.einsum(
            "gvs,gsl->gvl", tile_group, virt_rows, preferred_element_type=jnp.float32
        )
        aux_index = meta_group[:, 0]
        return (
            (occ_total.at[aux_index].add(occ_term), virt_total.at[aux_index].add(virt_term)),
            None,
        )

    start_totals = (
        jnp.zeros((aux_count, width_here, tile_side), jnp.float32),
        jnp.zeros((aux_count, tile_side, width_here), jnp.float32),
    )
    (occ_total, virt_total), _ = lax.scan(add_group, start_totals, (got_tiles, got_meta))
    occ_done, virt_done = (
        lax.psum_scatter(occ_total, "layer", scatter_dimension=1, tiled=True),
        lax.psum_scatter(virt_total, "layer", scatter_dimension=2, tiled=True),
    )
    mesh_count = row_count * layer_count
    thin_rows = tile_side // mesh_count
    stack_count = mesh_count // col_count
    narrow = occ_done.shape[1]
    occ_five = occ_done.reshape(aux_count, 1, col_count, thin_rows, tile_side)
    virt_five = virt_done.reshape(aux_count, stack_count, col_count, thin_rows, narrow)
    occ_moved, virt_moved = (
        lax.all_to_all(occ_five, "col", split_axis=2, concat_axis=1, tiled=True),
        lax.all_to_all(virt_five, "col", split_axis=2, concat_axis=1, tiled=True),
    )
    virt_four = virt_moved.reshape(aux_count, mesh_count, thin_rows, narrow)
    virt_back = lax.all_to_all(virt_four, ("row", "layer"), split_axis=1, concat_axis=3, tiled=True)
    occ_final = occ_moved.reshape(aux_count, col_count, thin_rows, tile_side)
    virt_final = virt_back.reshape(aux_count, thin_rows, col_count, tile_side)
    chi_part = jnp.einsum(
        "pcji,qjci->pq",
        occ_final,
        virt_final,
        precision=lax.Precision.HIGHEST,
        preferred_element_type=jnp.float32,
    )
    return lax.psum(chi_part, ("row", "col", "layer"))


def solution(mesh):
    in_specs = (
        P(("col", "layer"), None, None),
        P(("col", "layer")),
        P(("col", "layer")),
        P(("col", "layer")),
        P(("col", "layer")),
        P("layer", "row"),
        P("layer", "row"),
    )
    out_specs = P()
    side_of = (mesh.shape["row"], mesh.shape["col"], mesh.shape["layer"])
    return jax.shard_map(
        on_slice if side_of == (4, 2, 4) else on_device, mesh=mesh, in_specs=in_specs, out_specs=out_specs, check_vma=False
    )
```

```python
import jax
import jax.numpy as jnp
from jax import lax
from jax.experimental import pallas as pl
from jax.experimental.pallas import tpu as pltpu
from jax.sharding import PartitionSpec as P

NP = 24
MESH = pl.DeviceIdType.MESH
VMEM_LIMIT = 40 * 1024 * 1024
STEPS = 8
OFFSETS = ((1, 0), (0, 3), (0, 1), (1, 2), (1, 1), (1, 3), (0, 2))


def place():
    row, col, layer = lax.axis_index("row"), lax.axis_index("col"), lax.axis_index("layer")
    return row // 2, row % 2, col, layer


def exchange_kernel(cap, layer_blocks, list_hbm, blocks_hbm, occ_hbm, virt_hbm, tiles_ref, meta_out, green_ref,
                    blocks_ref, own_green, list_ref, code_ref, codes, meta_ref, send_buf, load_sem, meta_send, meta_recv, tile_send, tile_recv,
                    y_send, y_recv, core_send, core_recv, green_send, green_recv):
    y, core, col, layer = place()
    row = 2 * y + core
    across = 2 * (1 - y) + core
    sibling = 2 * y + 1 - core
    me = col * 4 + layer
    part = cap // 4
    side = blocks_ref.shape[1]
    half = own_green.shape[0]
    own_rows = pl.ds(pl.multiple_of(core * half, half), half)

    load_list = pltpu.make_async_copy(list_hbm, list_ref, load_sem.at[0])
    load_codes = pltpu.make_async_copy(code_ref, codes, load_sem.at[1])
    load_blocks = pltpu.make_async_copy(blocks_hbm, blocks_ref, load_sem.at[2])
    load_list.start()
    load_blocks.start()

    def load_own(source):
        return pltpu.make_async_copy(source, green_ref.at[own_rows], load_sem.at[3])

    def load_other(source):
        return pltpu.make_async_copy(source, own_green, load_sem.at[4])

    @pl.when(core == 0)
    def _():
        load_other(virt_hbm).start()
        load_own(occ_hbm).start()

    @pl.when(core == 1)
    def _():
        load_other(occ_hbm).start()
        load_own(virt_hbm).start()

    layers_by = (layer, layer + 1 - 2 * (layer % 2), (layer + 2) % 4, 3 - layer)
    barrier = pltpu.get_barrier_semaphore()
    peers = [(row, 1 - col if dc else col, layers_by[dl]) for dc, dl in OFFSETS]
    for peer in peers + [(across, col, layer), (sibling, col, layer)]:
        pl.semaphore_signal(barrier, inc=1, device_id=peer, device_id_type=MESH)
    load_list.wait()
    aux_list, row_list, col_list, ext_list = (list_ref[i:i + 1, :] for i in range(4))
    layer_list = sum((col_list >= edge * layer_blocks).astype(jnp.int32) for edge in range(1, 4))
    square = (8, 128)
    lane = lax.broadcasted_iota(jnp.int32, square, 1)
    owned = jnp.broadcast_to(row_list * 4 + layer_list, square) == lax.broadcasted_iota(jnp.int32, square, 0)
    rank = owned.astype(jnp.int32)
    step = 1
    while step < 128:
        rank += jnp.where(lane >= step, pltpu.roll(rank, step, 1), 0)
        step *= 2
    tile_code = lane * 256 + jnp.broadcast_to(ext_list, square)
    meta_code = jnp.broadcast_to(aux_list * 256 + col_list - layer_list * layer_blocks, square)
    tile_slots = jnp.zeros(square, jnp.int32)
    meta_slots = jnp.zeros(square, jnp.int32)
    for j in range(cap):
        here = jnp.logical_and(owned, rank == j + 1)
        tile_slots += jnp.where(lane == j, jnp.sum(jnp.where(here, tile_code, 0), axis=1, keepdims=True), 0)
        meta_slots += jnp.where(lane == j, jnp.sum(jnp.where(here, meta_code, 0), axis=1, keepdims=True), 0)
    code_ref[...] = tile_slots
    load_codes.start()
    for o in range(8):
        meta_ref[o] = jnp.broadcast_to(meta_slots[o:o + 1, :], square)

    pl.semaphore_wait(barrier, len(peers) + 2)

    greens = pltpu.make_async_remote_copy(
        src_ref=own_green, dst_ref=green_ref.at[own_rows], send_sem=green_send, recv_sem=green_recv,
        device_id=(sibling, col, layer), device_id_type=MESH)
    lanes = lax.broadcasted_iota(jnp.int32, (side, side), 1)

    def packed(owner, j):
        pick = codes[owner, row * part + j]
        tile = blocks_ref[pick // 256]
        return jnp.where(lanes < pick % 256, tile.astype(jnp.float32), 0.0).astype(tile.dtype)

    def owner_of(peer):
        return peer[1] * 4 + peer[2]

    def pack(k):
        for j in range(part):
            send_buf[k, j] = packed(owner_of(peers[k]), j)

    tile_copies = [pltpu.make_async_remote_copy(
        src_ref=send_buf.at[k], dst_ref=tiles_ref.at[row, me], send_sem=tile_send.at[k],
        recv_sem=tile_recv.at[k], device_id=peer, device_id_type=MESH) for k, peer in enumerate(peers)]
    meta_copies = [pltpu.make_async_remote_copy(
        src_ref=meta_ref.at[owner_of(peer)], dst_ref=meta_out.at[me], send_sem=meta_send.at[k],
        recv_sem=meta_recv.at[k], device_id=peer, device_id_type=MESH) for k, peer in enumerate(peers)]

    def forward(quarter, source, send, recv, k, target):
        copy = pltpu.make_async_remote_copy(
            src_ref=tiles_ref.at[quarter, source], dst_ref=tiles_ref.at[quarter, source],
            send_sem=send.at[k], recv_sem=recv.at[k], device_id=(target, col, layer), device_id_type=MESH)
        copy.start()
        return copy

    sources = [owner_of(peer) for peer in peers] + [me]
    order = [7] + list(range(7))
    to_y, to_core = {}, {}
    window = 4
    load_codes.wait()
    load_blocks.wait()

    def send(k):
        pack(k)
        tile_copies[k].start()

    send(0)
    for j in range(part):
        tiles_ref[row, me, j] = packed(me, j)
    to_y[7] = forward(row, me, y_send, y_recv, 7, across)
    to_core[7] = forward(row, me, core_send, core_recv, 7, sibling)
    for k in range(1, window):
        send(k)
    load_other(virt_hbm).wait()
    greens.start()
    for copy in meta_copies:
        copy.start()
    meta_out[me] = meta_ref[me]

    for k in range(window, 7):
        pack(k)
    for k in range(7):
        if k + window < 7:
            tile_copies[k].wait_send()
            tile_copies[k + window].start()
        tile_copies[k].wait_recv()
        to_y[k] = forward(row, sources[k], y_send, y_recv, k, across)
        to_core[k] = forward(row, sources[k], core_send, core_recv, k, sibling)
        if k >= 1:
            e = order[k - 1]
            to_y[e].wait_recv()
            to_core[8 + e] = forward(across, sources[e], core_send, core_recv, 8 + e, sibling)

    for e in order[6:]:
        to_y[e].wait_recv()
        to_core[8 + e] = forward(across, sources[e], core_send, core_recv, 8 + e, sibling)
    load_own(occ_hbm).wait()
    greens.wait()
    for k in range(7):
        if k + window >= 7:
            tile_copies[k].wait_send()
        meta_copies[k].wait()
    for k in order:
        to_y[k].wait_send()
        to_core[k].wait()
        to_core[8 + k].wait()


def product_kernel(cap, meta_ref, tiles_ref, green_ref, total_ref):
    part = cap // 4
    side = tiles_ref.shape[-1]
    total_ref[...] = jnp.zeros_like(total_ref)

    def add_all(flipped):
        @pl.loop(0, tiles_ref.shape[0] * tiles_ref.shape[1] // 2)
        def _(i):
            terms = []
            for h in range(2):
                n = 2 * i + h
                quarter, source = n // tiles_ref.shape[1], n % tiles_ref.shape[1]
                for j in range(part):
                    code = meta_ref[source, 0, quarter * part + j]
                    start = pl.multiple_of((code % 256) * side, side)
                    pair = (tiles_ref[quarter, source, j], green_ref[:, pl.ds(start, side)])
                    terms.append((code // 256, lax.dot_general(
                        *(pair[::-1] if flipped else pair), (((1,), (1,)), ((), ())),
                        preferred_element_type=jnp.float32)))
            for aux, term in terms:
                total_ref[aux] += term

    core = lax.axis_index("row") % 2
    pl.when(core == 0)(lambda: add_all(False))
    pl.when(core == 1)(lambda: add_all(True))


def pair_kernel(total_ref, chi_ref, right_in, left_in, done, occ_in, virt_in, plane_in, line_in,
                right_send, right_recv, left_send, left_recv, occ_send, occ_recv, virt_send, virt_recv,
                plane_send, plane_recv, line_send, line_recv):
    y, core, x, z = place()
    row = 2 * y + core
    count = total_ref.shape[0]
    rows = right_in.shape[1]
    thin = rows // 2
    steps = STEPS
    size = count // steps
    diagonal = x == y
    end = jnp.logical_or(z == 0, z == 3)

    def device(number):
        return (2 * (number // 4) + number % 2, (number // 2) % 2, z)

    mine = 4 * y + 2 * x + core
    barrier = pltpu.get_barrier_semaphore()
    for k in range(1, 4):
        pl.semaphore_signal(barrier, inc=1, device_id=(row, x, (z + k) % 4), device_id_type=MESH)
    for k in range(1, 8):
        pl.semaphore_signal(barrier, inc=1, device_id=device((mine + k) % 8), device_id_type=MESH)
    pl.semaphore_wait(barrier, 10)

    def chunk(c):
        return pl.ds(c * size, size)

    def right(c, source):
        return pltpu.make_async_remote_copy(
            src_ref=source, dst_ref=right_in.at[chunk(c)], send_sem=right_send.at[c], recv_sem=right_recv.at[c],
            device_id=(row, x, (z + 1) % 4), device_id_type=MESH)

    def left(c, source):
        return pltpu.make_async_remote_copy(
            src_ref=source, dst_ref=left_in.at[chunk(c)], send_sem=left_send.at[c], recv_sem=left_recv.at[c],
            device_id=(row, x, (z + 3) % 4), device_id_type=MESH)

    def pass_right(c):
        right(c, right_in.at[chunk(c)]).wait_recv()
        right_in[chunk(c)] += total_ref[chunk(c), rows:]
        right(c, right_in.at[chunk(c)]).start()

    def pass_left(c):
        left(c, left_in.at[chunk(c)]).wait_recv()
        left_in[chunk(c)] += total_ref[chunk(c), :rows]
        left(c, left_in.at[chunk(c)]).start()

    def occ_copy(c):
        return pltpu.make_async_remote_copy(
            src_ref=done.at[chunk(c), thin:], dst_ref=occ_in.at[chunk(c)], send_sem=occ_send.at[c],
            recv_sem=occ_recv.at[c], device_id=(2 * y + 1 - core, x, z), device_id_type=MESH)

    def virt_copy(c, kk):
        return pltpu.make_async_remote_copy(
            src_ref=done.at[chunk(c), kk * thin:(kk + 1) * thin], dst_ref=virt_in.at[chunk(c)],
            send_sem=virt_send.at[c, kk], recv_sem=virt_recv.at[c], device_id=(2 * x + kk, y, z),
            device_id_type=MESH)

    def hand_out(c):
        @pl.when(core == 0)
        def _():
            occ_copy(c).start()
            occ_in[chunk(c)] = done[chunk(c), :thin]

        @pl.when(core == 1)
        def _():
            virt_copy(c, 0).start()

            @pl.when(diagonal)
            def _():
                virt_in[chunk(c)] = done[chunk(c), thin:]

            @pl.when(jnp.logical_not(diagonal))
            def _():
                virt_copy(c, 1).start()

    lag = 6

    @pl.when(z == 0)
    def _():
        for c in range(steps + lag):
            if c < steps:
                if c >= 3:
                    right(c - 3, total_ref.at[chunk(c - 3), rows:]).wait_send()
                right(c, total_ref.at[chunk(c), rows:]).start()
            if c >= lag:
                e = c - lag
                left(e, left_in.at[chunk(e)]).wait_recv()
                done[chunk(e)] = left_in[chunk(e)] + total_ref[chunk(e), :rows]
                hand_out(e)
        for c in range(steps - 3, steps):
            right(c, total_ref.at[chunk(c), rows:]).wait_send()

    @pl.when(z == 3)
    def _():
        for c in range(steps + lag):
            if c < steps:
                if c >= 3:
                    left(c - 3, total_ref.at[chunk(c - 3), :rows]).wait_send()
                left(c, total_ref.at[chunk(c), :rows]).start()
            if c >= lag:
                e = c - lag
                right(e, right_in.at[chunk(e)]).wait_recv()
                done[chunk(e)] = right_in[chunk(e)] + total_ref[chunk(e), rows:]
                hand_out(e)
        for c in range(steps - 3, steps):
            left(c, total_ref.at[chunk(c), :rows]).wait_send()

    def relay(near, far):
        for c in range(steps + 2):
            if c < steps:
                near(c)
            if c >= 2:
                far(c - 2)

    pl.when(z == 1)(lambda: relay(pass_right, pass_left))
    pl.when(z == 2)(lambda: relay(pass_left, pass_right))

    @pl.when(jnp.logical_not(end))
    def _():
        for c in range(steps):
            right(c, right_in.at[chunk(c)]).wait_send()
            left(c, left_in.at[chunk(c)]).wait_send()

    def plane(k):
        return pltpu.make_async_remote_copy(
            src_ref=plane_in.at[mine], dst_ref=plane_in.at[mine], send_sem=plane_send.at[k],
            recv_sem=plane_recv.at[k], device_id=device((mine + k) % 8), device_id_type=MESH)

    def line(which, k):
        return pltpu.make_async_remote_copy(
            src_ref=line_in.at[which], dst_ref=line_in.at[which], send_sem=line_send.at[k],
            recv_sem=line_recv.at[which], device_id=(row, x, (z + k) % 4), device_id_type=MESH)

    @pl.when(end)
    def _():
        for c in range(steps):
            @pl.when(core == 1)
            def _():
                occ_copy(c).wait_recv()

            @pl.when(jnp.logical_not(jnp.logical_and(diagonal, core == 1)))
            def _():
                virt_copy(c, 0).wait_recv()
        def halves(ref, i):
            values = jnp.concatenate([ref[:, i, :], ref[:, i + 1, :]], axis=1)
            high = values.astype(jnp.bfloat16)
            low = (values - high.astype(jnp.float32)).astype(jnp.bfloat16)
            return jnp.concatenate([high.astype(jnp.float32), low.astype(jnp.float32)], axis=0).astype(jnp.bfloat16)

        both = jnp.zeros((2 * count, 2 * count), jnp.float32)
        for i in range(0, thin, 2):
            both += lax.dot_general(halves(occ_in, i), halves(virt_in, i), (((1,), (1,)), ((), ())),
                                    preferred_element_type=jnp.float32)
        chi = (both[:count, :count] + both[count:, count:]) + (both[:count, count:] + both[count:, :count])
        plane_in[mine] = jnp.pad(chi, ((0, 0), (0, 128 - count)))
        for k in range(1, 8):
            plane(k).start()
        for k in range(1, 8):
            plane(k).wait_recv()
        summed = plane_in[0]
        for k in range(1, 8):
            summed += plane_in[k]

        @pl.when(z == 0)
        def _():
            line_in[0] = summed
            for k in (3, 2, 1):
                line(0, k).start()

        @pl.when(z == 3)
        def _():
            line_in[1] = summed
            for k in (1, 2, 3):
                line(1, k).start()

    @pl.when(z > 0)
    def _():
        line(0, 1).wait_recv()

    @pl.when(z < 3)
    def _():
        line(1, 1).wait_recv()

    chi_ref[...] = (line_in[0] + line_in[1])[:, :count]

    @pl.when(end)
    def _():
        for k in range(1, 8):
            plane(k).wait_send()
        for k in range(1, 4):
            line(0, k).wait_send()
        for c in range(steps):
            @pl.when(core == 0)
            def _():
                occ_copy(c).wait_send()

            @pl.when(core == 1)
            def _():
                virt_copy(c, 0).wait_send()

                @pl.when(jnp.logical_not(diagonal))
                def _():
                    virt_copy(c, 1).wait_send()


def on_slice(blocks, block_aux, block_row, block_col, extents, occ_green, virt_green):
    held, side, _ = blocks.shape
    owners = 8
    cap = held // owners + 1
    depth, width = occ_green.shape
    smem, vmem = pl.BlockSpec(memory_space=pltpu.SMEM), pl.BlockSpec(memory_space=pltpu.VMEM)
    f32, i32 = jnp.float32, jnp.int32
    dma = pltpu.SemaphoreType.DMA

    def bind(kernel, *sizes):
        def run(*refs):
            kernel(*sizes, *refs)
        return run

    lists = jnp.pad(jnp.stack([block_aux, block_row, block_col, extents]), ((0, 4), (0, 128 - held)),
                    constant_values=1 << 20)
    part = cap // 4
    tiles, meta, green = pl.pallas_call(
        bind(exchange_kernel, cap, depth // side),
        out_shape=(
            jax.ShapeDtypeStruct((4, owners, part, side, side), blocks.dtype),
            jax.ShapeDtypeStruct((owners, 8, 128), i32),
            jax.ShapeDtypeStruct((2 * width, depth), occ_green.dtype),
        ),
        in_specs=[pl.BlockSpec(memory_space=pl.ANY)] * 4,
        out_specs=(vmem, vmem, vmem),
        scratch_shapes=[
            pltpu.VMEM(blocks.shape, blocks.dtype),
            pltpu.VMEM((width, depth), occ_green.dtype),
            pltpu.VMEM((8, 128), i32),
            pltpu.VMEM((8, 128), i32),
            pltpu.SMEM((8, 128), i32),
            pltpu.VMEM((owners, 8, 128), i32),
            pltpu.VMEM((7, part, side, side), blocks.dtype),
            dma((5,)),
            dma((7,)), dma((7,)), dma((7,)), dma((7,)), dma((8,)), dma((8,)), dma((16,)), dma((16,)),
            dma(()), dma(()),
        ],
        compiler_params=pltpu.CompilerParams(collective_id=0, has_side_effects=True, vmem_limit_bytes=59 * 1024 * 1024),
        name="exchange",
    )(lists, blocks, occ_green.T, virt_green.T)
    total = pl.pallas_call(
        bind(product_kernel, cap),
        out_shape=jax.ShapeDtypeStruct((NP, side, 2 * width), f32),
        in_specs=[smem, vmem, vmem],
        out_specs=vmem,
        compiler_params=pltpu.CompilerParams(vmem_limit_bytes=VMEM_LIMIT),
        name="product",
    )(meta, tiles, green)
    rows, part_rows = side // 2, side // 4
    return pl.pallas_call(
        pair_kernel,
        out_shape=jax.ShapeDtypeStruct((NP, NP), f32),
        in_specs=[vmem],
        out_specs=vmem,
        scratch_shapes=[
            pltpu.VMEM((NP, rows, side), f32),
            pltpu.VMEM((NP, rows, side), f32),
            pltpu.VMEM((NP, rows, side), f32),
            pltpu.VMEM((NP, part_rows, side), f32),
            pltpu.VMEM((NP, part_rows, side), f32),
            pltpu.VMEM((8, NP, 128), f32),
            pltpu.VMEM((2, NP, 128), f32),
            dma((STEPS,)), dma((STEPS,)), dma((STEPS,)), dma((STEPS,)), dma((STEPS,)), dma((STEPS,)),
            dma((STEPS, 2)), dma((STEPS,)), dma((8,)), dma((8,)), dma((4,)), dma((2,)),
        ],
        compiler_params=pltpu.CompilerParams(collective_id=1, has_side_effects=True, vmem_limit_bytes=VMEM_LIMIT),
        name="pair",
    )(total)


def on_device(blocks, block_aux, block_row, block_col, extents, occ_green, virt_green):
    row_count = lax.axis_size("row")
    col_count = lax.axis_size("col")
    layer_count = lax.axis_size("layer")
    held_count = blocks.shape[0]
    tile_side = blocks.shape[1]
    aux_count = NP
    owner_count = col_count * layer_count
    capacity = max(2, held_count // owner_count + 1)
    layer_blocks = occ_green.shape[0] // tile_side
    columns = jnp.arange(tile_side, dtype=jnp.int32)
    masked_tiles = jnp.where(
        columns[None, None, :] < extents[:, None, None], blocks, jnp.zeros((), blocks.dtype)
    )
    layer_of = block_col // layer_blocks
    target = block_row * layer_count + layer_of
    kept_col = block_col - layer_of * layer_blocks
    marked = (target[:, None] == jnp.arange(owner_count, dtype=jnp.int32)[None, :]).astype(
        jnp.int32
    )
    earlier = jnp.cumsum(marked, axis=0) - marked
    placed = target * capacity + jnp.sum(earlier * marked, axis=1)
    send_tiles = (
        jnp.zeros((owner_count * capacity, tile_side, tile_side), blocks.dtype)
        .at[placed]
        .set(masked_tiles)
    )
    send_meta = (
        jnp.zeros((owner_count * capacity, 2), jnp.int32)
        .at[placed]
        .set(jnp.stack([block_aux, kept_col], axis=1))
    )
    send_tiles = send_tiles.reshape(col_count, layer_count, capacity, tile_side, tile_side)
    send_meta = send_meta.reshape(col_count, layer_count, capacity, 2)
    total_slots = col_count * layer_count * capacity
    got_tiles, got_meta = (
        lax.all_to_all(
            send_tiles.reshape(total_slots, tile_side, tile_side),
            ("col", "layer"),
            split_axis=0,
            concat_axis=0,
            tiled=True,
        ),
        lax.all_to_all(
            send_meta.reshape(total_slots, 2),
            ("col", "layer"),
            split_axis=0,
            concat_axis=0,
            tiled=True,
        ),
    )
    group_size = col_count * capacity
    got_tiles = got_tiles.reshape(layer_count, group_size, tile_side, tile_side)
    got_meta = got_meta.reshape(layer_count, group_size, 2)
    occ_cols, virt_cols = (occ_green, virt_green)
    width_here = occ_cols.shape[1]
    offsets = jnp.arange(tile_side, dtype=jnp.int32)

    def add_group(totals, record):
        occ_total, virt_total = totals
        tile_group, meta_group = record
        row_index = meta_group[:, 1][:, None] * tile_side + offsets[None, :]
        occ_rows = occ_cols[row_index]
        virt_rows = virt_cols[row_index]
        occ_term = jnp.einsum(
            "gsv,gls->gvl", occ_rows, tile_group, preferred_element_type=jnp.float32
        )
        virt_term = jnp.einsum(
            "gvs,gsl->gvl", tile_group, virt_rows, preferred_element_type=jnp.float32
        )
        aux_index = meta_group[:, 0]
        return (
            (occ_total.at[aux_index].add(occ_term), virt_total.at[aux_index].add(virt_term)),
            None,
        )

    start_totals = (
        jnp.zeros((aux_count, width_here, tile_side), jnp.float32),
        jnp.zeros((aux_count, tile_side, width_here), jnp.float32),
    )
    (occ_total, virt_total), _ = lax.scan(add_group, start_totals, (got_tiles, got_meta))
    occ_done, virt_done = (
        lax.psum_scatter(occ_total, "layer", scatter_dimension=1, tiled=True),
        lax.psum_scatter(virt_total, "layer", scatter_dimension=2, tiled=True),
    )
    mesh_count = row_count * layer_count
    thin_rows = tile_side // mesh_count
    stack_count = mesh_count // col_count
    narrow = occ_done.shape[1]
    occ_five = occ_done.reshape(aux_count, 1, col_count, thin_rows, tile_side)
    virt_five = virt_done.reshape(aux_count, stack_count, col_count, thin_rows, narrow)
    occ_moved, virt_moved = (
        lax.all_to_all(occ_five, "col", split_axis=2, concat_axis=1, tiled=True),
        lax.all_to_all(virt_five, "col", split_axis=2, concat_axis=1, tiled=True),
    )
    virt_four = virt_moved.reshape(aux_count, mesh_count, thin_rows, narrow)
    virt_back = lax.all_to_all(virt_four, ("row", "layer"), split_axis=1, concat_axis=3, tiled=True)
    occ_final = occ_moved.reshape(aux_count, col_count, thin_rows, tile_side)
    virt_final = virt_back.reshape(aux_count, thin_rows, col_count, tile_side)
    chi_part = jnp.einsum(
        "pcji,qjci->pq",
        occ_final,
        virt_final,
        precision=lax.Precision.HIGHEST,
        preferred_element_type=jnp.float32,
    )
    return lax.psum(chi_part, ("row", "col", "layer"))


def solution(mesh):
    in_specs = (
        P(("col", "layer"), None, None),
        P(("col", "layer")),
        P(("col", "layer")),
        P(("col", "layer")),
        P(("col", "layer")),
        P("layer", "row"),
        P("layer", "row"),
    )
    out_specs = P()
    side_of = (mesh.shape["row"], mesh.shape["col"], mesh.shape["layer"])
    return jax.shard_map(
        on_slice if side_of == (4, 2, 4) else on_device, mesh=mesh, in_specs=in_specs, out_specs=out_specs, check_vma=False
    )
```

```python
import jax
import jax.numpy as jnp
from jax import lax
from jax.experimental import pallas as pl
from jax.experimental.pallas import tpu as pltpu
from jax.sharding import PartitionSpec as P

NP = 24
MESH = pl.DeviceIdType.MESH
VMEM_LIMIT = 59 * 1024 * 1024
STEPS = 12
OFFSETS = ((1, 0), (0, 3), (0, 1), (1, 2), (1, 1), (1, 3), (0, 2))


def place():
    row, col, layer = lax.axis_index("row"), lax.axis_index("col"), lax.axis_index("layer")
    return row // 2, row % 2, col, layer


def exchange_kernel(cap, layer_blocks, list_hbm, blocks_hbm, occ_hbm, virt_hbm, tiles_ref, meta_out, green_ref,
                    blocks_ref, own_green, list_ref, code_ref, codes, meta_ref, send_buf, load_sem, meta_send, meta_recv, tile_send, tile_recv,
                    y_send, y_recv, core_send, core_recv, green_send, green_recv):
    y, core, col, layer = place()
    row = 2 * y + core
    across = 2 * (1 - y) + core
    sibling = 2 * y + 1 - core
    me = col * 4 + layer
    part = cap // 4
    side = blocks_ref.shape[1]
    half = own_green.shape[0]
    own_rows = pl.ds(pl.multiple_of(core * half, half), half)

    load_list = pltpu.make_async_copy(list_hbm, list_ref, load_sem.at[0])
    load_codes = pltpu.make_async_copy(code_ref, codes, load_sem.at[1])
    load_blocks = pltpu.make_async_copy(blocks_hbm, blocks_ref, load_sem.at[2])
    load_list.start()
    load_blocks.start()

    def load_own(source):
        return pltpu.make_async_copy(source, green_ref.at[own_rows], load_sem.at[3])

    def load_other(source):
        return pltpu.make_async_copy(source, own_green, load_sem.at[4])

    @pl.when(core == 0)
    def _():
        load_other(virt_hbm).start()
        load_own(occ_hbm).start()

    @pl.when(core == 1)
    def _():
        load_other(occ_hbm).start()
        load_own(virt_hbm).start()

    layers_by = (layer, layer + 1 - 2 * (layer % 2), (layer + 2) % 4, 3 - layer)
    barrier = pltpu.get_barrier_semaphore()
    peers = [(row, 1 - col if dc else col, layers_by[dl]) for dc, dl in OFFSETS]
    for peer in peers + [(across, col, layer), (sibling, col, layer)]:
        pl.semaphore_signal(barrier, inc=1, device_id=peer, device_id_type=MESH)
    load_list.wait()
    aux_list, row_list, col_list, ext_list = (list_ref[i:i + 1, :] for i in range(4))
    layer_list = sum((col_list >= edge * layer_blocks).astype(jnp.int32) for edge in range(1, 4))
    square = (8, 128)
    lane = lax.broadcasted_iota(jnp.int32, square, 1)
    owned = jnp.broadcast_to(row_list * 4 + layer_list, square) == lax.broadcasted_iota(jnp.int32, square, 0)
    rank = owned.astype(jnp.int32)
    step = 1
    while step < 128:
        rank += jnp.where(lane >= step, pltpu.roll(rank, step, 1), 0)
        step *= 2
    tile_code = lane * 256 + jnp.broadcast_to(ext_list, square)
    meta_code = jnp.broadcast_to(aux_list * 256 + col_list - layer_list * layer_blocks, square)
    tile_slots = jnp.zeros(square, jnp.int32)
    meta_slots = jnp.zeros(square, jnp.int32)
    for j in range(cap):
        here = jnp.logical_and(owned, rank == j + 1)
        tile_slots += jnp.where(lane == j, jnp.sum(jnp.where(here, tile_code, 0), axis=1, keepdims=True), 0)
        meta_slots += jnp.where(lane == j, jnp.sum(jnp.where(here, meta_code, 0), axis=1, keepdims=True), 0)
    code_ref[...] = tile_slots
    load_codes.start()
    for o in range(8):
        meta_ref[o] = jnp.broadcast_to(meta_slots[o:o + 1, :], square)

    pl.semaphore_wait(barrier, len(peers) + 2)

    greens = pltpu.make_async_remote_copy(
        src_ref=own_green, dst_ref=green_ref.at[own_rows], send_sem=green_send, recv_sem=green_recv,
        device_id=(sibling, col, layer), device_id_type=MESH)
    lanes = lax.broadcasted_iota(jnp.int32, (side, side), 1)

    def packed(owner, j):
        pick = codes[owner, row * part + j]
        tile = blocks_ref[pick // 256]
        return jnp.where(lanes < pick % 256, tile.astype(jnp.float32), 0.0).astype(tile.dtype)

    def owner_of(peer):
        return peer[1] * 4 + peer[2]

    def pack(k):
        for j in range(part):
            send_buf[k, j] = packed(owner_of(peers[k]), j)

    tile_copies = [pltpu.make_async_remote_copy(
        src_ref=send_buf.at[k], dst_ref=tiles_ref.at[row, me], send_sem=tile_send.at[k],
        recv_sem=tile_recv.at[k], device_id=peer, device_id_type=MESH) for k, peer in enumerate(peers)]
    meta_copies = [pltpu.make_async_remote_copy(
        src_ref=meta_ref.at[owner_of(peer)], dst_ref=meta_out.at[me], send_sem=meta_send.at[k],
        recv_sem=meta_recv.at[k], device_id=peer, device_id_type=MESH) for k, peer in enumerate(peers)]

    def forward(quarter, source, send, recv, k, target):
        copy = pltpu.make_async_remote_copy(
            src_ref=tiles_ref.at[quarter, source], dst_ref=tiles_ref.at[quarter, source],
            send_sem=send.at[k], recv_sem=recv.at[k], device_id=(target, col, layer), device_id_type=MESH)
        copy.start()
        return copy

    sources = [owner_of(peer) for peer in peers] + [me]
    order = [7] + list(range(7))
    to_y, to_core = {}, {}
    window = 4
    load_codes.wait()
    load_blocks.wait()

    def send(k):
        pack(k)
        tile_copies[k].start()

    send(0)
    for j in range(part):
        tiles_ref[row, me, j] = packed(me, j)
    to_y[7] = forward(row, me, y_send, y_recv, 7, across)
    to_core[7] = forward(row, me, core_send, core_recv, 7, sibling)
    for k in range(1, window):
        send(k)
    load_other(virt_hbm).wait()
    greens.start()
    for copy in meta_copies:
        copy.start()
    meta_out[me] = meta_ref[me]

    for k in range(window, 7):
        pack(k)
    for k in range(7):
        if k + window < 7:
            tile_copies[k].wait_send()
            tile_copies[k + window].start()
        tile_copies[k].wait_recv()
        to_y[k] = forward(row, sources[k], y_send, y_recv, k, across)
        to_core[k] = forward(row, sources[k], core_send, core_recv, k, sibling)
        if k >= 1:
            e = order[k - 1]
            to_y[e].wait_recv()
            to_core[8 + e] = forward(across, sources[e], core_send, core_recv, 8 + e, sibling)

    for e in order[6:]:
        to_y[e].wait_recv()
        to_core[8 + e] = forward(across, sources[e], core_send, core_recv, 8 + e, sibling)
    load_own(occ_hbm).wait()
    greens.wait()
    for k in range(7):
        if k + window >= 7:
            tile_copies[k].wait_send()
        meta_copies[k].wait()
    for k in order:
        to_y[k].wait_send()
        to_core[k].wait()
        to_core[8 + k].wait()


def product_kernel(cap, meta_ref, tiles_hbm, green_hbm, total_ref, tiles_ref, green_ref, load_sem):
    part = cap // 4
    side = tiles_ref.shape[-1]
    load_green = pltpu.make_async_copy(green_hbm, green_ref, load_sem.at[4])
    load_green.start()
    loads = [pltpu.make_async_copy(tiles_hbm.at[q], tiles_ref.at[q], load_sem.at[q]) for q in range(4)]
    for load in loads:
        load.start()
    total_ref[...] = jnp.zeros_like(total_ref)
    load_green.wait()

    def add_all(flipped):
        for quarter in range(4):
            loads[quarter].wait()
            add_quarter(flipped, quarter)

    def add_quarter(flipped, quarter):
        @pl.loop(0, tiles_ref.shape[1] // 2)
        def _(i):
            terms = []
            for h in range(2):
                source = 2 * i + h
                for j in range(part):
                    code = meta_ref[source, 0, quarter * part + j]
                    start = pl.multiple_of((code % 256) * side, side)
                    pair = (tiles_ref[quarter, source, j], green_ref[:, pl.ds(start, side)])
                    terms.append((code // 256, lax.dot_general(
                        *(pair[::-1] if flipped else pair), (((1,), (1,)), ((), ())),
                        preferred_element_type=jnp.float32)))
            for aux, term in terms:
                total_ref[aux] += term

    core = lax.axis_index("row") % 2
    pl.when(core == 0)(lambda: add_all(False))
    pl.when(core == 1)(lambda: add_all(True))


def pair_kernel(total_hbm, chi_ref, total_ref, load_sem, right_in, left_in, done, occ_in, virt_in, plane_in, line_in,
                right_send, right_recv, left_send, left_recv, occ_send, occ_recv, virt_send, virt_recv,
                plane_send, plane_recv, line_send, line_recv):
    y, core, x, z = place()
    row = 2 * y + core
    count = total_ref.shape[0]
    rows = right_in.shape[1]
    thin = rows // 2
    steps = STEPS
    size = count // steps
    diagonal = x == y
    end = jnp.logical_or(z == 0, z == 3)

    def device(number):
        return (2 * (number // 4) + number % 2, (number // 2) % 2, z)

    mine = 4 * y + 2 * x + core
    load_total = pltpu.make_async_copy(total_hbm, total_ref, load_sem)
    load_total.start()
    barrier = pltpu.get_barrier_semaphore()
    for k in range(1, 4):
        pl.semaphore_signal(barrier, inc=1, device_id=(row, x, (z + k) % 4), device_id_type=MESH)
    for k in range(1, 8):
        pl.semaphore_signal(barrier, inc=1, device_id=device((mine + k) % 8), device_id_type=MESH)
    pl.semaphore_wait(barrier, 10)
    load_total.wait()

    def chunk(c):
        return pl.ds(c * size, size)

    def right(c, source):
        return pltpu.make_async_remote_copy(
            src_ref=source, dst_ref=right_in.at[chunk(c)], send_sem=right_send.at[c], recv_sem=right_recv.at[c],
            device_id=(row, x, (z + 1) % 4), device_id_type=MESH)

    def left(c, source):
        return pltpu.make_async_remote_copy(
            src_ref=source, dst_ref=left_in.at[chunk(c)], send_sem=left_send.at[c], recv_sem=left_recv.at[c],
            device_id=(row, x, (z + 3) % 4), device_id_type=MESH)

    def pass_right(c):
        right(c, right_in.at[chunk(c)]).wait_recv()
        right_in[chunk(c)] += total_ref[chunk(c), rows:]
        right(c, right_in.at[chunk(c)]).start()

    def pass_left(c):
        left(c, left_in.at[chunk(c)]).wait_recv()
        left_in[chunk(c)] += total_ref[chunk(c), :rows]
        left(c, left_in.at[chunk(c)]).start()

    def occ_copy(c):
        return pltpu.make_async_remote_copy(
            src_ref=done.at[chunk(c), thin:], dst_ref=occ_in.at[chunk(c)], send_sem=occ_send.at[c],
            recv_sem=occ_recv.at[c], device_id=(2 * y + 1 - core, x, z), device_id_type=MESH)

    def virt_copy(c, kk):
        return pltpu.make_async_remote_copy(
            src_ref=done.at[chunk(c), kk * thin:(kk + 1) * thin], dst_ref=virt_in.at[chunk(c)],
            send_sem=virt_send.at[c, kk], recv_sem=virt_recv.at[c], device_id=(2 * x + kk, y, z),
            device_id_type=MESH)

    def hand_out(c):
        @pl.when(core == 0)
        def _():
            occ_copy(c).start()
            occ_in[chunk(c)] = done[chunk(c), :thin]

        @pl.when(core == 1)
        def _():
            virt_copy(c, 0).start()

            @pl.when(diagonal)
            def _():
                virt_in[chunk(c)] = done[chunk(c), thin:]

            @pl.when(jnp.logical_not(diagonal))
            def _():
                virt_copy(c, 1).start()

    lag = 7

    @pl.when(z == 0)
    def _():
        for c in range(steps + lag):
            if c < steps:
                if c >= 3:
                    right(c - 3, total_ref.at[chunk(c - 3), rows:]).wait_send()
                right(c, total_ref.at[chunk(c), rows:]).start()
            if c >= lag:
                e = c - lag
                left(e, left_in.at[chunk(e)]).wait_recv()
                done[chunk(e)] = left_in[chunk(e)] + total_ref[chunk(e), :rows]
                hand_out(e)
        for c in range(steps - 3, steps):
            right(c, total_ref.at[chunk(c), rows:]).wait_send()

    @pl.when(z == 3)
    def _():
        for c in range(steps + lag):
            if c < steps:
                if c >= 3:
                    left(c - 3, total_ref.at[chunk(c - 3), :rows]).wait_send()
                left(c, total_ref.at[chunk(c), :rows]).start()
            if c >= lag:
                e = c - lag
                right(e, right_in.at[chunk(e)]).wait_recv()
                done[chunk(e)] = right_in[chunk(e)] + total_ref[chunk(e), rows:]
                hand_out(e)
        for c in range(steps - 3, steps):
            left(c, total_ref.at[chunk(c), :rows]).wait_send()

    def relay(near, far):
        for c in range(steps + 3):
            if c < steps:
                near(c)
            if c >= 3:
                far(c - 3)

    pl.when(z == 1)(lambda: relay(pass_right, pass_left))
    pl.when(z == 2)(lambda: relay(pass_left, pass_right))

    @pl.when(jnp.logical_not(end))
    def _():
        for c in range(steps):
            right(c, right_in.at[chunk(c)]).wait_send()
            left(c, left_in.at[chunk(c)]).wait_send()

    def plane(k):
        return pltpu.make_async_remote_copy(
            src_ref=plane_in.at[mine], dst_ref=plane_in.at[mine], send_sem=plane_send.at[k],
            recv_sem=plane_recv.at[k], device_id=device((mine + k) % 8), device_id_type=MESH)

    def line(which, k):
        return pltpu.make_async_remote_copy(
            src_ref=line_in.at[which], dst_ref=line_in.at[which], send_sem=line_send.at[k],
            recv_sem=line_recv.at[which], device_id=(row, x, (z + k) % 4), device_id_type=MESH)

    @pl.when(end)
    def _():
        for c in range(steps):
            @pl.when(core == 1)
            def _():
                occ_copy(c).wait_recv()

            @pl.when(jnp.logical_not(jnp.logical_and(diagonal, core == 1)))
            def _():
                virt_copy(c, 0).wait_recv()
        def halves(ref, i):
            values = jnp.concatenate([ref[:, i, :], ref[:, i + 1, :]], axis=1)
            high = values.astype(jnp.bfloat16)
            low = (values - high.astype(jnp.float32)).astype(jnp.bfloat16)
            return jnp.concatenate([high.astype(jnp.float32), low.astype(jnp.float32)], axis=0).astype(jnp.bfloat16)

        both = jnp.zeros((2 * count, 2 * count), jnp.float32)
        for i in range(0, thin, 2):
            both += lax.dot_general(halves(occ_in, i), halves(virt_in, i), (((1,), (1,)), ((), ())),
                                    preferred_element_type=jnp.float32)
        chi = (both[:count, :count] + both[count:, count:]) + (both[:count, count:] + both[count:, :count])
        plane_in[mine] = jnp.pad(chi, ((0, 0), (0, 128 - count)))
        for k in range(1, 8):
            plane(k).start()
        for k in range(1, 8):
            plane(k).wait_recv()
        summed = plane_in[0]
        for k in range(1, 8):
            summed += plane_in[k]

        @pl.when(z == 0)
        def _():
            line_in[0] = summed
            for k in (3, 2, 1):
                line(0, k).start()

        @pl.when(z == 3)
        def _():
            line_in[1] = summed
            for k in (1, 2, 3):
                line(1, k).start()

    @pl.when(z > 0)
    def _():
        line(0, 1).wait_recv()

    @pl.when(z < 3)
    def _():
        line(1, 1).wait_recv()

    chi_ref[...] = (line_in[0] + line_in[1])[:, :count]

    @pl.when(end)
    def _():
        for k in range(1, 8):
            plane(k).wait_send()
        for k in range(1, 4):
            line(0, k).wait_send()
        for c in range(steps):
            @pl.when(core == 0)
            def _():
                occ_copy(c).wait_send()

            @pl.when(core == 1)
            def _():
                virt_copy(c, 0).wait_send()

                @pl.when(jnp.logical_not(diagonal))
                def _():
                    virt_copy(c, 1).wait_send()


def on_slice(blocks, block_aux, block_row, block_col, extents, occ_green, virt_green):
    held, side, _ = blocks.shape
    owners = 8
    cap = held // owners + 1
    depth, width = occ_green.shape
    smem, vmem = pl.BlockSpec(memory_space=pltpu.SMEM), pl.BlockSpec(memory_space=pltpu.VMEM)
    f32, i32 = jnp.float32, jnp.int32
    dma = pltpu.SemaphoreType.DMA

    def bind(kernel, *sizes):
        def run(*refs):
            kernel(*sizes, *refs)
        return run

    lists = jnp.pad(jnp.stack([block_aux, block_row, block_col, extents]), ((0, 4), (0, 128 - held)),
                    constant_values=1 << 20)
    part = cap // 4
    tiles, meta, green = pl.pallas_call(
        bind(exchange_kernel, cap, depth // side),
        out_shape=(
            jax.ShapeDtypeStruct((4, owners, part, side, side), blocks.dtype),
            jax.ShapeDtypeStruct((owners, 8, 128), i32),
            jax.ShapeDtypeStruct((2 * width, depth), occ_green.dtype),
        ),
        in_specs=[pl.BlockSpec(memory_space=pl.ANY)] * 4,
        out_specs=(vmem, vmem, vmem),
        scratch_shapes=[
            pltpu.VMEM(blocks.shape, blocks.dtype),
            pltpu.VMEM((width, depth), occ_green.dtype),
            pltpu.VMEM((8, 128), i32),
            pltpu.VMEM((8, 128), i32),
            pltpu.SMEM((8, 128), i32),
            pltpu.VMEM((owners, 8, 128), i32),
            pltpu.VMEM((7, part, side, side), blocks.dtype),
            dma((5,)),
            dma((7,)), dma((7,)), dma((7,)), dma((7,)), dma((8,)), dma((8,)), dma((16,)), dma((16,)),
            dma(()), dma(()),
        ],
        compiler_params=pltpu.CompilerParams(collective_id=0, has_side_effects=True, vmem_limit_bytes=VMEM_LIMIT),
        name="exchange",
    )(lists, blocks, occ_green.T, virt_green.T)
    total = pl.pallas_call(
        bind(product_kernel, cap),
        out_shape=jax.ShapeDtypeStruct((NP, side, 2 * width), f32),
        in_specs=[smem, pl.BlockSpec(memory_space=pl.ANY), pl.BlockSpec(memory_space=pl.ANY)],
        out_specs=vmem,
        scratch_shapes=[
            pltpu.VMEM((4, owners, part, side, side), blocks.dtype),
            pltpu.VMEM((2 * width, depth), occ_green.dtype),
            dma((5,)),
        ],
        compiler_params=pltpu.CompilerParams(vmem_limit_bytes=VMEM_LIMIT),
        name="product",
    )(meta, tiles, green)
    rows, part_rows = side // 2, side // 4
    return pl.pallas_call(
        pair_kernel,
        out_shape=jax.ShapeDtypeStruct((NP, NP), f32),
        in_specs=[pl.BlockSpec(memory_space=pl.ANY)],
        out_specs=vmem,
        scratch_shapes=[
            pltpu.VMEM((NP, side, side), f32),
            dma(()),
            pltpu.VMEM((NP, rows, side), f32),
            pltpu.VMEM((NP, rows, side), f32),
            pltpu.VMEM((NP, rows, side), f32),
            pltpu.VMEM((NP, part_rows, side), f32),
            pltpu.VMEM((NP, part_rows, side), f32),
            pltpu.VMEM((8, NP, 128), f32),
            pltpu.VMEM((2, NP, 128), f32),
            dma((STEPS,)), dma((STEPS,)), dma((STEPS,)), dma((STEPS,)), dma((STEPS,)), dma((STEPS,)),
            dma((STEPS, 2)), dma((STEPS,)), dma((8,)), dma((8,)), dma((4,)), dma((2,)),
        ],
        compiler_params=pltpu.CompilerParams(collective_id=1, has_side_effects=True, vmem_limit_bytes=VMEM_LIMIT),
        name="pair",
    )(total)


def on_device(blocks, block_aux, block_row, block_col, extents, occ_green, virt_green):
    row_count = lax.axis_size("row")
    col_count = lax.axis_size("col")
    layer_count = lax.axis_size("layer")
    held_count = blocks.shape[0]
    tile_side = blocks.shape[1]
    aux_count = NP
    owner_count = col_count * layer_count
    capacity = max(2, held_count // owner_count + 1)
    layer_blocks = occ_green.shape[0] // tile_side
    columns = jnp.arange(tile_side, dtype=jnp.int32)
    masked_tiles = jnp.where(
        columns[None, None, :] < extents[:, None, None], blocks, jnp.zeros((), blocks.dtype)
    )
    layer_of = block_col // layer_blocks
    target = block_row * layer_count + layer_of
    kept_col = block_col - layer_of * layer_blocks
    marked = (target[:, None] == jnp.arange(owner_count, dtype=jnp.int32)[None, :]).astype(
        jnp.int32
    )
    earlier = jnp.cumsum(marked, axis=0) - marked
    placed = target * capacity + jnp.sum(earlier * marked, axis=1)
    send_tiles = (
        jnp.zeros((owner_count * capacity, tile_side, tile_side), blocks.dtype)
        .at[placed]
        .set(masked_tiles)
    )
    send_meta = (
        jnp.zeros((owner_count * capacity, 2), jnp.int32)
        .at[placed]
        .set(jnp.stack([block_aux, kept_col], axis=1))
    )
    send_tiles = send_tiles.reshape(col_count, layer_count, capacity, tile_side, tile_side)
    send_meta = send_meta.reshape(col_count, layer_count, capacity, 2)
    total_slots = col_count * layer_count * capacity
    got_tiles, got_meta = (
        lax.all_to_all(
            send_tiles.reshape(total_slots, tile_side, tile_side),
            ("col", "layer"),
            split_axis=0,
            concat_axis=0,
            tiled=True,
        ),
        lax.all_to_all(
            send_meta.reshape(total_slots, 2),
            ("col", "layer"),
            split_axis=0,
            concat_axis=0,
            tiled=True,
        ),
    )
    group_size = col_count * capacity
    got_tiles = got_tiles.reshape(layer_count, group_size, tile_side, tile_side)
    got_meta = got_meta.reshape(layer_count, group_size, 2)
    occ_cols, virt_cols = (occ_green, virt_green)
    width_here = occ_cols.shape[1]
    offsets = jnp.arange(tile_side, dtype=jnp.int32)

    def add_group(totals, record):
        occ_total, virt_total = totals
        tile_group, meta_group = record
        row_index = meta_group[:, 1][:, None] * tile_side + offsets[None, :]
        occ_rows = occ_cols[row_index]
        virt_rows = virt_cols[row_index]
        occ_term = jnp.einsum(
            "gsv,gls->gvl", occ_rows, tile_group, preferred_element_type=jnp.float32
        )
        virt_term = jnp.einsum(
            "gvs,gsl->gvl", tile_group, virt_rows, preferred_element_type=jnp.float32
        )
        aux_index = meta_group[:, 0]
        return (
            (occ_total.at[aux_index].add(occ_term), virt_total.at[aux_index].add(virt_term)),
            None,
        )

    start_totals = (
        jnp.zeros((aux_count, width_here, tile_side), jnp.float32),
        jnp.zeros((aux_count, tile_side, width_here), jnp.float32),
    )
    (occ_total, virt_total), _ = lax.scan(add_group, start_totals, (got_tiles, got_meta))
    occ_done, virt_done = (
        lax.psum_scatter(occ_total, "layer", scatter_dimension=1, tiled=True),
        lax.psum_scatter(virt_total, "layer", scatter_dimension=2, tiled=True),
    )
    mesh_count = row_count * layer_count
    thin_rows = tile_side // mesh_count
    stack_count = mesh_count // col_count
    narrow = occ_done.shape[1]
    occ_five = occ_done.reshape(aux_count, 1, col_count, thin_rows, tile_side)
    virt_five = virt_done.reshape(aux_count, stack_count, col_count, thin_rows, narrow)
    occ_moved, virt_moved = (
        lax.all_to_all(occ_five, "col", split_axis=2, concat_axis=1, tiled=True),
        lax.all_to_all(virt_five, "col", split_axis=2, concat_axis=1, tiled=True),
    )
    virt_four = virt_moved.reshape(aux_count, mesh_count, thin_rows, narrow)
    virt_back = lax.all_to_all(virt_four, ("row", "layer"), split_axis=1, concat_axis=3, tiled=True)
    occ_final = occ_moved.reshape(aux_count, col_count, thin_rows, tile_side)
    virt_final = virt_back.reshape(aux_count, thin_rows, col_count, tile_side)
    chi_part = jnp.einsum(
        "pcji,qjci->pq",
        occ_final,
        virt_final,
        precision=lax.Precision.HIGHEST,
        preferred_element_type=jnp.float32,
    )
    return lax.psum(chi_part, ("row", "col", "layer"))


def solution(mesh):
    in_specs = (
        P(("col", "layer"), None, None),
        P(("col", "layer")),
        P(("col", "layer")),
        P(("col", "layer")),
        P(("col", "layer")),
        P("layer", "row"),
        P("layer", "row"),
    )
    out_specs = P()
    side_of = (mesh.shape["row"], mesh.shape["col"], mesh.shape["layer"])
    return jax.shard_map(
        on_slice if side_of == (4, 2, 4) else on_device, mesh=mesh, in_specs=in_specs, out_specs=out_specs, check_vma=False
    )
```

```python
import jax
import jax.numpy as jnp
from jax import lax
from jax.experimental import pallas as pl
from jax.experimental.pallas import tpu as pltpu
from jax.sharding import PartitionSpec as P

NP = 24
MESH = pl.DeviceIdType.MESH
VMEM_LIMIT = 59 * 1024 * 1024
STEPS = 12
OFFSETS = ((1, 0), (0, 3), (0, 1), (1, 2), (1, 1), (1, 3), (0, 2))


def place():
    row, col, layer = lax.axis_index("row"), lax.axis_index("col"), lax.axis_index("layer")
    return row // 2, row % 2, col, layer


def exchange_kernel(cap, layer_blocks, list_hbm, blocks_hbm, occ_hbm, virt_hbm, tiles_ref, meta_out, green_ref,
                    blocks_ref, own_green, list_ref, code_ref, codes, meta_ref, send_buf, load_sem, meta_send, meta_recv, tile_send, tile_recv,
                    y_send, y_recv, core_send, core_recv, green_send, green_recv):
    y, core, col, layer = place()
    row = 2 * y + core
    across = 2 * (1 - y) + core
    sibling = 2 * y + 1 - core
    me = col * 4 + layer
    part = cap // 4
    side = blocks_ref.shape[1]
    half = own_green.shape[0]
    own_rows = pl.ds(pl.multiple_of(core * half, half), half)

    load_list = pltpu.make_async_copy(list_hbm, list_ref, load_sem.at[0])
    load_codes = pltpu.make_async_copy(code_ref, codes, load_sem.at[1])
    load_blocks = pltpu.make_async_copy(blocks_hbm, blocks_ref, load_sem.at[2])
    load_list.start()
    load_blocks.start()

    def load_own(source):
        return pltpu.make_async_copy(source, green_ref.at[own_rows], load_sem.at[3])

    def load_other(source):
        return pltpu.make_async_copy(source, own_green, load_sem.at[4])

    @pl.when(core == 0)
    def _():
        load_other(virt_hbm).start()
        load_own(occ_hbm).start()

    @pl.when(core == 1)
    def _():
        load_other(occ_hbm).start()
        load_own(virt_hbm).start()

    layers_by = (layer, layer + 1 - 2 * (layer % 2), (layer + 2) % 4, 3 - layer)
    barrier = pltpu.get_barrier_semaphore()
    peers = [(row, 1 - col if dc else col, layers_by[dl]) for dc, dl in OFFSETS]
    for peer in peers + [(across, col, layer), (sibling, col, layer)]:
        pl.semaphore_signal(barrier, inc=1, device_id=peer, device_id_type=MESH)
    load_list.wait()
    aux_list, row_list, col_list, ext_list = (list_ref[i:i + 1, :] for i in range(4))
    layer_list = sum((col_list >= edge * layer_blocks).astype(jnp.int32) for edge in range(1, 4))
    square = (8, 128)
    lane = lax.broadcasted_iota(jnp.int32, square, 1)
    owned = jnp.broadcast_to(row_list * 4 + layer_list, square) == lax.broadcasted_iota(jnp.int32, square, 0)
    rank = owned.astype(jnp.int32)
    step = 1
    while step < 128:
        rank += jnp.where(lane >= step, pltpu.roll(rank, step, 1), 0)
        step *= 2
    tile_code = lane * 256 + jnp.broadcast_to(ext_list, square)
    meta_code = jnp.broadcast_to(aux_list * 256 + col_list - layer_list * layer_blocks, square)
    tile_slots = jnp.zeros(square, jnp.int32)
    meta_slots = jnp.zeros(square, jnp.int32)
    for j in range(cap):
        here = jnp.logical_and(owned, rank == j + 1)
        tile_slots += jnp.where(lane == j, jnp.sum(jnp.where(here, tile_code, 0), axis=1, keepdims=True), 0)
        meta_slots += jnp.where(lane == j, jnp.sum(jnp.where(here, meta_code, 0), axis=1, keepdims=True), 0)
    code_ref[...] = tile_slots
    load_codes.start()
    for o in range(8):
        meta_ref[o] = jnp.broadcast_to(meta_slots[o:o + 1, :], square)

    pl.semaphore_wait(barrier, len(peers) + 2)

    greens = pltpu.make_async_remote_copy(
        src_ref=own_green, dst_ref=green_ref.at[own_rows], send_sem=green_send, recv_sem=green_recv,
        device_id=(sibling, col, layer), device_id_type=MESH)
    lanes = lax.broadcasted_iota(jnp.int32, (side, side), 1)

    def packed(owner, j):
        pick = codes[owner, row * part + j]
        tile = blocks_ref[pick // 256]
        return jnp.where(lanes < pick % 256, tile.astype(jnp.float32), 0.0).astype(tile.dtype)

    def owner_of(peer):
        return peer[1] * 4 + peer[2]

    def pack(k):
        for j in range(part):
            send_buf[k, j] = packed(owner_of(peers[k]), j)

    tile_copies = [pltpu.make_async_remote_copy(
        src_ref=send_buf.at[k], dst_ref=tiles_ref.at[row, me], send_sem=tile_send.at[k],
        recv_sem=tile_recv.at[k], device_id=peer, device_id_type=MESH) for k, peer in enumerate(peers)]
    meta_copies = [pltpu.make_async_remote_copy(
        src_ref=meta_ref.at[owner_of(peer)], dst_ref=meta_out.at[me], send_sem=meta_send.at[k],
        recv_sem=meta_recv.at[k], device_id=peer, device_id_type=MESH) for k, peer in enumerate(peers)]

    def forward(quarter, source, send, recv, k, target):
        copy = pltpu.make_async_remote_copy(
            src_ref=tiles_ref.at[quarter, source], dst_ref=tiles_ref.at[quarter, source],
            send_sem=send.at[k], recv_sem=recv.at[k], device_id=(target, col, layer), device_id_type=MESH)
        copy.start()
        return copy

    sources = [owner_of(peer) for peer in peers] + [me]
    order = [7] + list(range(7))
    to_y, to_core = {}, {}
    window = 4
    load_codes.wait()
    load_blocks.wait()

    def send(k):
        pack(k)
        tile_copies[k].start()

    send(0)
    for j in range(part):
        tiles_ref[row, me, j] = packed(me, j)
    to_y[7] = forward(row, me, y_send, y_recv, 7, across)
    to_core[7] = forward(row, me, core_send, core_recv, 7, sibling)
    for k in range(1, window):
        send(k)
    load_other(virt_hbm).wait()
    greens.start()
    for copy in meta_copies:
        copy.start()
    meta_out[me] = meta_ref[me]

    for k in range(window, 7):
        pack(k)
    for k in range(7):
        if k + window < 7:
            tile_copies[k].wait_send()
            tile_copies[k + window].start()
        tile_copies[k].wait_recv()
        to_y[k] = forward(row, sources[k], y_send, y_recv, k, across)
        to_core[k] = forward(row, sources[k], core_send, core_recv, k, sibling)
        if k >= 3:
            e = order[k - 3]
            to_y[e].wait_recv()
            to_core[8 + e] = forward(across, sources[e], core_send, core_recv, 8 + e, sibling)

    for e in order[4:]:
        to_y[e].wait_recv()
        to_core[8 + e] = forward(across, sources[e], core_send, core_recv, 8 + e, sibling)
    load_own(occ_hbm).wait()
    greens.wait()
    for k in range(7):
        if k + window >= 7:
            tile_copies[k].wait_send()
        meta_copies[k].wait()
    for k in order:
        to_y[k].wait_send()
        to_core[k].wait()
        to_core[8 + k].wait()


def product_kernel(cap, meta_ref, tiles_hbm, green_hbm, total_ref, tiles_ref, green_ref, load_sem):
    part = cap // 4
    side = tiles_ref.shape[-1]
    load_green = pltpu.make_async_copy(green_hbm, green_ref, load_sem.at[4])
    load_green.start()
    loads = [pltpu.make_async_copy(tiles_hbm.at[q], tiles_ref.at[q], load_sem.at[q]) for q in range(4)]
    for load in loads:
        load.start()
    total_ref[...] = jnp.zeros_like(total_ref)
    load_green.wait()

    def add_all(flipped):
        for quarter in range(4):
            loads[quarter].wait()
            add_quarter(flipped, quarter)

    def add_quarter(flipped, quarter):
        @pl.loop(0, tiles_ref.shape[1] // 2)
        def _(i):
            terms = []
            for h in range(2):
                source = 2 * i + h
                for j in range(part):
                    code = meta_ref[source, 0, quarter * part + j]
                    start = pl.multiple_of((code % 256) * side, side)
                    pair = (tiles_ref[quarter, source, j], green_ref[:, pl.ds(start, side)])
                    terms.append((code // 256, lax.dot_general(
                        *(pair[::-1] if flipped else pair), (((1,), (1,)), ((), ())),
                        preferred_element_type=jnp.float32)))
            for aux, term in terms:
                total_ref[aux] += term

    core = lax.axis_index("row") % 2
    pl.when(core == 0)(lambda: add_all(False))
    pl.when(core == 1)(lambda: add_all(True))


def pair_kernel(total_hbm, chi_ref, total_ref, load_sem, right_in, left_in, done, occ_in, virt_in, plane_in, line_in,
                right_send, right_recv, left_send, left_recv, occ_send, occ_recv, virt_send, virt_recv,
                plane_send, plane_recv, line_send, line_recv):
    y, core, x, z = place()
    row = 2 * y + core
    count = total_ref.shape[0]
    rows = right_in.shape[1]
    thin = rows // 2
    steps = STEPS
    size = count // steps
    diagonal = x == y
    end = jnp.logical_or(z == 0, z == 3)

    def device(number):
        return (2 * (number // 4) + number % 2, (number // 2) % 2, z)

    mine = 4 * y + 2 * x + core
    load_total = pltpu.make_async_copy(total_hbm, total_ref, load_sem)
    load_total.start()
    barrier = pltpu.get_barrier_semaphore()
    for k in range(1, 4):
        pl.semaphore_signal(barrier, inc=1, device_id=(row, x, (z + k) % 4), device_id_type=MESH)
    for k in range(1, 8):
        pl.semaphore_signal(barrier, inc=1, device_id=device((mine + k) % 8), device_id_type=MESH)
    pl.semaphore_wait(barrier, 10)
    load_total.wait()

    def chunk(c):
        return pl.ds(c * size, size)

    def right(c, source):
        return pltpu.make_async_remote_copy(
            src_ref=source, dst_ref=right_in.at[chunk(c)], send_sem=right_send.at[c], recv_sem=right_recv.at[c],
            device_id=(row, x, (z + 1) % 4), device_id_type=MESH)

    def left(c, source):
        return pltpu.make_async_remote_copy(
            src_ref=source, dst_ref=left_in.at[chunk(c)], send_sem=left_send.at[c], recv_sem=left_recv.at[c],
            device_id=(row, x, (z + 3) % 4), device_id_type=MESH)

    def pass_right(c):
        right(c, right_in.at[chunk(c)]).wait_recv()
        right_in[chunk(c)] += total_ref[chunk(c), rows:]
        right(c, right_in.at[chunk(c)]).start()

    def pass_left(c):
        left(c, left_in.at[chunk(c)]).wait_recv()
        left_in[chunk(c)] += total_ref[chunk(c), :rows]
        left(c, left_in.at[chunk(c)]).start()

    def occ_copy(c):
        return pltpu.make_async_remote_copy(
            src_ref=done.at[chunk(c), thin:], dst_ref=occ_in.at[chunk(c)], send_sem=occ_send.at[c],
            recv_sem=occ_recv.at[c], device_id=(2 * y + 1 - core, x, z), device_id_type=MESH)

    def virt_copy(c, kk):
        return pltpu.make_async_remote_copy(
            src_ref=done.at[chunk(c), kk * thin:(kk + 1) * thin], dst_ref=virt_in.at[chunk(c)],
            send_sem=virt_send.at[c, kk], recv_sem=virt_recv.at[c], device_id=(2 * x + kk, y, z),
            device_id_type=MESH)

    def hand_out(c):
        @pl.when(core == 0)
        def _():
            occ_copy(c).start()
            occ_in[chunk(c)] = done[chunk(c), :thin]

        @pl.when(core == 1)
        def _():
            virt_copy(c, 0).start()

            @pl.when(diagonal)
            def _():
                virt_in[chunk(c)] = done[chunk(c), thin:]

            @pl.when(jnp.logical_not(diagonal))
            def _():
                virt_copy(c, 1).start()

    lag = 7

    @pl.when(z == 0)
    def _():
        for c in range(steps + lag):
            if c < steps:
                if c >= 5:
                    right(c - 5, total_ref.at[chunk(c - 5), rows:]).wait_send()
                right(c, total_ref.at[chunk(c), rows:]).start()
            if c >= lag:
                e = c - lag
                left(e, left_in.at[chunk(e)]).wait_recv()
                done[chunk(e)] = left_in[chunk(e)] + total_ref[chunk(e), :rows]
                hand_out(e)
        for c in range(steps - 5, steps):
            right(c, total_ref.at[chunk(c), rows:]).wait_send()

    @pl.when(z == 3)
    def _():
        for c in range(steps + lag):
            if c < steps:
                if c >= 5:
                    left(c - 5, total_ref.at[chunk(c - 5), :rows]).wait_send()
                left(c, total_ref.at[chunk(c), :rows]).start()
            if c >= lag:
                e = c - lag
                right(e, right_in.at[chunk(e)]).wait_recv()
                done[chunk(e)] = right_in[chunk(e)] + total_ref[chunk(e), rows:]
                hand_out(e)
        for c in range(steps - 5, steps):
            left(c, total_ref.at[chunk(c), :rows]).wait_send()

    def relay(near, far):
        for c in range(steps + 3):
            if c < steps:
                near(c)
            if c >= 3:
                far(c - 3)

    pl.when(z == 1)(lambda: relay(pass_right, pass_left))
    pl.when(z == 2)(lambda: relay(pass_left, pass_right))

    @pl.when(jnp.logical_not(end))
    def _():
        for c in range(steps):
            right(c, right_in.at[chunk(c)]).wait_send()
            left(c, left_in.at[chunk(c)]).wait_send()

    def plane(k):
        return pltpu.make_async_remote_copy(
            src_ref=plane_in.at[mine], dst_ref=plane_in.at[mine], send_sem=plane_send.at[k],
            recv_sem=plane_recv.at[k], device_id=device((mine + k) % 8), device_id_type=MESH)

    def line(which, k):
        return pltpu.make_async_remote_copy(
            src_ref=line_in.at[which], dst_ref=line_in.at[which], send_sem=line_send.at[k],
            recv_sem=line_recv.at[which], device_id=(row, x, (z + k) % 4), device_id_type=MESH)

    @pl.when(end)
    def _():
        for c in range(steps):
            @pl.when(core == 1)
            def _():
                occ_copy(c).wait_recv()

            @pl.when(jnp.logical_not(jnp.logical_and(diagonal, core == 1)))
            def _():
                virt_copy(c, 0).wait_recv()
        def halves(ref, i):
            values = jnp.concatenate([ref[:, i, :], ref[:, i + 1, :]], axis=1)
            high = values.astype(jnp.bfloat16)
            low = (values - high.astype(jnp.float32)).astype(jnp.bfloat16)
            return jnp.concatenate([high.astype(jnp.float32), low.astype(jnp.float32)], axis=0).astype(jnp.bfloat16)

        both = jnp.zeros((2 * count, 2 * count), jnp.float32)
        for i in range(0, thin, 2):
            both += lax.dot_general(halves(occ_in, i), halves(virt_in, i), (((1,), (1,)), ((), ())),
                                    preferred_element_type=jnp.float32)
        chi = (both[:count, :count] + both[count:, count:]) + (both[:count, count:] + both[count:, :count])
        plane_in[mine] = jnp.pad(chi, ((0, 0), (0, 128 - count)))
        for k in range(1, 8):
            plane(k).start()
        for k in range(1, 8):
            plane(k).wait_recv()
        summed = plane_in[0]
        for k in range(1, 8):
            summed += plane_in[k]

        @pl.when(z == 0)
        def _():
            line_in[0] = summed
            for k in (3, 2, 1):
                line(0, k).start()

        @pl.when(z == 3)
        def _():
            line_in[1] = summed
            for k in (1, 2, 3):
                line(1, k).start()

    @pl.when(z > 0)
    def _():
        line(0, 1).wait_recv()

    @pl.when(z < 3)
    def _():
        line(1, 1).wait_recv()

    chi_ref[...] = (line_in[0] + line_in[1])[:, :count]

    @pl.when(end)
    def _():
        for k in range(1, 8):
            plane(k).wait_send()
        for k in range(1, 4):
            line(0, k).wait_send()
        for c in range(steps):
            @pl.when(core == 0)
            def _():
                occ_copy(c).wait_send()

            @pl.when(core == 1)
            def _():
                virt_copy(c, 0).wait_send()

                @pl.when(jnp.logical_not(diagonal))
                def _():
                    virt_copy(c, 1).wait_send()


def on_slice(blocks, block_aux, block_row, block_col, extents, occ_green, virt_green):
    held, side, _ = blocks.shape
    owners = 8
    cap = held // owners + 1
    depth, width = occ_green.shape
    smem, vmem = pl.BlockSpec(memory_space=pltpu.SMEM), pl.BlockSpec(memory_space=pltpu.VMEM)
    f32, i32 = jnp.float32, jnp.int32
    dma = pltpu.SemaphoreType.DMA

    def bind(kernel, *sizes):
        def run(*refs):
            kernel(*sizes, *refs)
        return run

    lists = jnp.pad(jnp.stack([block_aux, block_row, block_col, extents]), ((0, 4), (0, 128 - held)),
                    constant_values=1 << 20)
    part = cap // 4
    tiles, meta, green = pl.pallas_call(
        bind(exchange_kernel, cap, depth // side),
        out_shape=(
            jax.ShapeDtypeStruct((4, owners, part, side, side), blocks.dtype),
            jax.ShapeDtypeStruct((owners, 8, 128), i32),
            jax.ShapeDtypeStruct((2 * width, depth), occ_green.dtype),
        ),
        in_specs=[pl.BlockSpec(memory_space=pl.ANY)] * 4,
        out_specs=(vmem, vmem, vmem),
        scratch_shapes=[
            pltpu.VMEM(blocks.shape, blocks.dtype),
            pltpu.VMEM((width, depth), occ_green.dtype),
            pltpu.VMEM((8, 128), i32),
            pltpu.VMEM((8, 128), i32),
            pltpu.SMEM((8, 128), i32),
            pltpu.VMEM((owners, 8, 128), i32),
            pltpu.VMEM((7, part, side, side), blocks.dtype),
            dma((5,)),
            dma((7,)), dma((7,)), dma((7,)), dma((7,)), dma((8,)), dma((8,)), dma((16,)), dma((16,)),
            dma(()), dma(()),
        ],
        compiler_params=pltpu.CompilerParams(collective_id=0, has_side_effects=True, vmem_limit_bytes=VMEM_LIMIT),
        name="exchange",
    )(lists, blocks, occ_green.T, virt_green.T)
    total = pl.pallas_call(
        bind(product_kernel, cap),
        out_shape=jax.ShapeDtypeStruct((NP, side, 2 * width), f32),
        in_specs=[smem, pl.BlockSpec(memory_space=pl.ANY), pl.BlockSpec(memory_space=pl.ANY)],
        out_specs=vmem,
        scratch_shapes=[
            pltpu.VMEM((4, owners, part, side, side), blocks.dtype),
            pltpu.VMEM((2 * width, depth), occ_green.dtype),
            dma((5,)),
        ],
        compiler_params=pltpu.CompilerParams(vmem_limit_bytes=VMEM_LIMIT),
        name="product",
    )(meta, tiles, green)
    rows, part_rows = side // 2, side // 4
    return pl.pallas_call(
        pair_kernel,
        out_shape=jax.ShapeDtypeStruct((NP, NP), f32),
        in_specs=[pl.BlockSpec(memory_space=pl.ANY)],
        out_specs=vmem,
        scratch_shapes=[
            pltpu.VMEM((NP, side, side), f32),
            dma(()),
            pltpu.VMEM((NP, rows, side), f32),
            pltpu.VMEM((NP, rows, side), f32),
            pltpu.VMEM((NP, rows, side), f32),
            pltpu.VMEM((NP, part_rows, side), f32),
            pltpu.VMEM((NP, part_rows, side), f32),
            pltpu.VMEM((8, NP, 128), f32),
            pltpu.VMEM((2, NP, 128), f32),
            dma((STEPS,)), dma((STEPS,)), dma((STEPS,)), dma((STEPS,)), dma((STEPS,)), dma((STEPS,)),
            dma((STEPS, 2)), dma((STEPS,)), dma((8,)), dma((8,)), dma((4,)), dma((2,)),
        ],
        compiler_params=pltpu.CompilerParams(collective_id=1, has_side_effects=True, vmem_limit_bytes=53 * 1024 * 1024),
        name="pair",
    )(total)


def on_device(blocks, block_aux, block_row, block_col, extents, occ_green, virt_green):
    row_count = lax.axis_size("row")
    col_count = lax.axis_size("col")
    layer_count = lax.axis_size("layer")
    held_count = blocks.shape[0]
    tile_side = blocks.shape[1]
    aux_count = NP
    owner_count = col_count * layer_count
    capacity = max(2, held_count // owner_count + 1)
    layer_blocks = occ_green.shape[0] // tile_side
    columns = jnp.arange(tile_side, dtype=jnp.int32)
    masked_tiles = jnp.where(
        columns[None, None, :] < extents[:, None, None], blocks, jnp.zeros((), blocks.dtype)
    )
    layer_of = block_col // layer_blocks
    target = block_row * layer_count + layer_of
    kept_col = block_col - layer_of * layer_blocks
    marked = (target[:, None] == jnp.arange(owner_count, dtype=jnp.int32)[None, :]).astype(
        jnp.int32
    )
    earlier = jnp.cumsum(marked, axis=0) - marked
    placed = target * capacity + jnp.sum(earlier * marked, axis=1)
    send_tiles = (
        jnp.zeros((owner_count * capacity, tile_side, tile_side), blocks.dtype)
        .at[placed]
        .set(masked_tiles)
    )
    send_meta = (
        jnp.zeros((owner_count * capacity, 2), jnp.int32)
        .at[placed]
        .set(jnp.stack([block_aux, kept_col], axis=1))
    )
    send_tiles = send_tiles.reshape(col_count, layer_count, capacity, tile_side, tile_side)
    send_meta = send_meta.reshape(col_count, layer_count, capacity, 2)
    total_slots = col_count * layer_count * capacity
    got_tiles, got_meta = (
        lax.all_to_all(
            send_tiles.reshape(total_slots, tile_side, tile_side),
            ("col", "layer"),
            split_axis=0,
            concat_axis=0,
            tiled=True,
        ),
        lax.all_to_all(
            send_meta.reshape(total_slots, 2),
            ("col", "layer"),
            split_axis=0,
            concat_axis=0,
            tiled=True,
        ),
    )
    group_size = col_count * capacity
    got_tiles = got_tiles.reshape(layer_count, group_size, tile_side, tile_side)
    got_meta = got_meta.reshape(layer_count, group_size, 2)
    occ_cols, virt_cols = (occ_green, virt_green)
    width_here = occ_cols.shape[1]
    offsets = jnp.arange(tile_side, dtype=jnp.int32)

    def add_group(totals, record):
        occ_total, virt_total = totals
        tile_group, meta_group = record
        row_index = meta_group[:, 1][:, None] * tile_side + offsets[None, :]
        occ_rows = occ_cols[row_index]
        virt_rows = virt_cols[row_index]
        occ_term = jnp.einsum(
            "gsv,gls->gvl", occ_rows, tile_group, preferred_element_type=jnp.float32
        )
        virt_term = jnp.einsum(
            "gvs,gsl->gvl", tile_group, virt_rows, preferred_element_type=jnp.float32
        )
        aux_index = meta_group[:, 0]
        return (
            (occ_total.at[aux_index].add(occ_term), virt_total.at[aux_index].add(virt_term)),
            None,
        )

    start_totals = (
        jnp.zeros((aux_count, width_here, tile_side), jnp.float32),
        jnp.zeros((aux_count, tile_side, width_here), jnp.float32),
    )
    (occ_total, virt_total), _ = lax.scan(add_group, start_totals, (got_tiles, got_meta))
    occ_done, virt_done = (
        lax.psum_scatter(occ_total, "layer", scatter_dimension=1, tiled=True),
        lax.psum_scatter(virt_total, "layer", scatter_dimension=2, tiled=True),
    )
    mesh_count = row_count * layer_count
    thin_rows = tile_side // mesh_count
    stack_count = mesh_count // col_count
    narrow = occ_done.shape[1]
    occ_five = occ_done.reshape(aux_count, 1, col_count, thin_rows, tile_side)
    virt_five = virt_done.reshape(aux_count, stack_count, col_count, thin_rows, narrow)
    occ_moved, virt_moved = (
        lax.all_to_all(occ_five, "col", split_axis=2, concat_axis=1, tiled=True),
        lax.all_to_all(virt_five, "col", split_axis=2, concat_axis=1, tiled=True),
    )
    virt_four = virt_moved.reshape(aux_count, mesh_count, thin_rows, narrow)
    virt_back = lax.all_to_all(virt_four, ("row", "layer"), split_axis=1, concat_axis=3, tiled=True)
    occ_final = occ_moved.reshape(aux_count, col_count, thin_rows, tile_side)
    virt_final = virt_back.reshape(aux_count, thin_rows, col_count, tile_side)
    chi_part = jnp.einsum(
        "pcji,qjci->pq",
        occ_final,
        virt_final,
        precision=lax.Precision.HIGHEST,
        preferred_element_type=jnp.float32,
    )
    return lax.psum(chi_part, ("row", "col", "layer"))


def solution(mesh):
    in_specs = (
        P(("col", "layer"), None, None),
        P(("col", "layer")),
        P(("col", "layer")),
        P(("col", "layer")),
        P(("col", "layer")),
        P("layer", "row"),
        P("layer", "row"),
    )
    out_specs = P()
    side_of = (mesh.shape["row"], mesh.shape["col"], mesh.shape["layer"])
    return jax.shard_map(
        on_slice if side_of == (4, 2, 4) else on_device, mesh=mesh, in_specs=in_specs, out_specs=out_specs, check_vma=False
    )
```

```python
import jax
import jax.numpy as jnp
from jax import lax
from jax.experimental import pallas as pl
from jax.experimental.pallas import tpu as pltpu
from jax.sharding import PartitionSpec as P

NP = 24
MESH = pl.DeviceIdType.MESH
VMEM_LIMIT = 59 * 1024 * 1024
STEPS = 12
OFFSETS = ((1, 0), (0, 3), (0, 1), (1, 2), (1, 1), (1, 3), (0, 2))


def place():
    row, col, layer = lax.axis_index("row"), lax.axis_index("col"), lax.axis_index("layer")
    return row // 2, row % 2, col, layer


def exchange_kernel(cap, layer_blocks, list_hbm, blocks_hbm, occ_hbm, virt_hbm, tiles_ref, meta_out, green_ref,
                    blocks_ref, own_green, list_ref, code_ref, codes, meta_ref, send_buf, load_sem, meta_send, meta_recv, tile_send, tile_recv,
                    y_send, y_recv, core_send, core_recv, green_send, green_recv):
    y, core, col, layer = place()
    row = 2 * y + core
    across = 2 * (1 - y) + core
    sibling = 2 * y + 1 - core
    me = col * 4 + layer
    part = cap // 4
    side = blocks_ref.shape[1]
    half = own_green.shape[0]
    own_rows = pl.ds(pl.multiple_of(core * half, half), half)

    load_list = pltpu.make_async_copy(list_hbm, list_ref, load_sem.at[0])
    load_codes = pltpu.make_async_copy(code_ref, codes, load_sem.at[1])
    load_blocks = pltpu.make_async_copy(blocks_hbm, blocks_ref, load_sem.at[2])
    load_list.start()
    load_blocks.start()

    def load_own(source):
        return pltpu.make_async_copy(source, green_ref.at[own_rows], load_sem.at[3])

    def load_other(source):
        return pltpu.make_async_copy(source, own_green, load_sem.at[4])

    @pl.when(core == 0)
    def _():
        load_other(virt_hbm).start()
        load_own(occ_hbm).start()

    @pl.when(core == 1)
    def _():
        load_other(occ_hbm).start()
        load_own(virt_hbm).start()

    layers_by = (layer, layer + 1 - 2 * (layer % 2), (layer + 2) % 4, 3 - layer)
    barrier = pltpu.get_barrier_semaphore()
    peers = [(row, 1 - col if dc else col, layers_by[dl]) for dc, dl in OFFSETS]
    for peer in peers + [(across, col, layer), (sibling, col, layer)]:
        pl.semaphore_signal(barrier, inc=1, device_id=peer, device_id_type=MESH)
    load_list.wait()
    aux_list, row_list, col_list, ext_list = (list_ref[i:i + 1, :] for i in range(4))
    layer_list = sum((col_list >= edge * layer_blocks).astype(jnp.int32) for edge in range(1, 4))
    square = (8, 128)
    lane = lax.broadcasted_iota(jnp.int32, square, 1)
    owned = jnp.broadcast_to(row_list * 4 + layer_list, square) == lax.broadcasted_iota(jnp.int32, square, 0)
    rank = owned.astype(jnp.int32)
    step = 1
    while step < 128:
        rank += jnp.where(lane >= step, pltpu.roll(rank, step, 1), 0)
        step *= 2
    tile_code = lane * 256 + jnp.broadcast_to(ext_list, square)
    meta_code = jnp.broadcast_to(aux_list * 256 + col_list - layer_list * layer_blocks, square)
    tile_slots = jnp.zeros(square, jnp.int32)
    meta_slots = jnp.zeros(square, jnp.int32)
    for j in range(cap):
        here = jnp.logical_and(owned, rank == j + 1)
        tile_slots += jnp.where(lane == j, jnp.sum(jnp.where(here, tile_code, 0), axis=1, keepdims=True), 0)
        meta_slots += jnp.where(lane == j, jnp.sum(jnp.where(here, meta_code, 0), axis=1, keepdims=True), 0)
    code_ref[...] = tile_slots
    load_codes.start()
    for o in range(8):
        meta_ref[o] = jnp.broadcast_to(meta_slots[o:o + 1, :], square)

    pl.semaphore_wait(barrier, len(peers) + 2)

    greens = pltpu.make_async_remote_copy(
        src_ref=own_green, dst_ref=green_ref.at[own_rows], send_sem=green_send, recv_sem=green_recv,
        device_id=(sibling, col, layer), device_id_type=MESH)
    lanes = lax.broadcasted_iota(jnp.int32, (side, side), 1)

    def packed(owner, j):
        pick = codes[owner, row * part + j]
        tile = blocks_ref[pick // 256]
        return jnp.where(lanes < pick % 256, tile.astype(jnp.float32), 0.0).astype(tile.dtype)

    def owner_of(peer):
        return peer[1] * 4 + peer[2]

    def pack(k):
        for j in range(part):
            send_buf[k, j] = packed(owner_of(peers[k]), j)

    tile_copies = [pltpu.make_async_remote_copy(
        src_ref=send_buf.at[k], dst_ref=tiles_ref.at[row, me], send_sem=tile_send.at[k],
        recv_sem=tile_recv.at[k], device_id=peer, device_id_type=MESH) for k, peer in enumerate(peers)]
    meta_copies = [pltpu.make_async_remote_copy(
        src_ref=meta_ref.at[owner_of(peer)], dst_ref=meta_out.at[me], send_sem=meta_send.at[k],
        recv_sem=meta_recv.at[k], device_id=peer, device_id_type=MESH) for k, peer in enumerate(peers)]

    def forward(quarter, source, send, recv, k, target):
        copy = pltpu.make_async_remote_copy(
            src_ref=tiles_ref.at[quarter, source], dst_ref=tiles_ref.at[quarter, source],
            send_sem=send.at[k], recv_sem=recv.at[k], device_id=(target, col, layer), device_id_type=MESH)
        copy.start()
        return copy

    sources = [owner_of(peer) for peer in peers] + [me]
    order = [7] + list(range(7))
    to_y, to_core = {}, {}
    window = 5
    load_codes.wait()
    load_blocks.wait()

    def send(k):
        pack(k)
        tile_copies[k].start()

    send(0)
    for j in range(part):
        tiles_ref[row, me, j] = packed(me, j)
    to_y[7] = forward(row, me, y_send, y_recv, 7, across)
    to_core[7] = forward(row, me, core_send, core_recv, 7, sibling)
    for k in range(1, window):
        send(k)
    load_other(virt_hbm).wait()
    greens.start()
    for copy in meta_copies:
        copy.start()
    meta_out[me] = meta_ref[me]

    for k in range(window, 7):
        pack(k)
    for k in range(7):
        if k + window < 7:
            tile_copies[k].wait_send()
            tile_copies[k + window].start()
        tile_copies[k].wait_recv()
        to_y[k] = forward(row, sources[k], y_send, y_recv, k, across)
        to_core[k] = forward(row, sources[k], core_send, core_recv, k, sibling)
        if k >= 3:
            e = order[k - 3]
            to_y[e].wait_recv()
            to_core[8 + e] = forward(across, sources[e], core_send, core_recv, 8 + e, sibling)

    for e in order[4:]:
        to_y[e].wait_recv()
        to_core[8 + e] = forward(across, sources[e], core_send, core_recv, 8 + e, sibling)
    load_own(occ_hbm).wait()
    greens.wait()
    for k in range(7):
        if k + window >= 7:
            tile_copies[k].wait_send()
        meta_copies[k].wait()
    for k in order:
        to_y[k].wait_send()
        to_core[k].wait()
        to_core[8 + k].wait()


def product_kernel(cap, meta_ref, tiles_hbm, green_hbm, total_ref, tiles_ref, green_ref, load_sem):
    part = cap // 4
    side = tiles_ref.shape[-1]
    load_green = pltpu.make_async_copy(green_hbm, green_ref, load_sem.at[4])
    load_green.start()
    loads = [pltpu.make_async_copy(tiles_hbm.at[q], tiles_ref.at[q], load_sem.at[q]) for q in range(4)]
    for load in loads:
        load.start()
    total_ref[...] = jnp.zeros_like(total_ref)
    load_green.wait()

    def add_all(flipped):
        for quarter in range(4):
            loads[quarter].wait()
            add_quarter(flipped, quarter)

    def add_quarter(flipped, quarter):
        @pl.loop(0, tiles_ref.shape[1] // 4)
        def _(i):
            terms = []
            for h in range(4):
                source = 4 * i + h
                for j in range(part):
                    code = meta_ref[source, 0, quarter * part + j]
                    start = pl.multiple_of((code % 256) * side, side)
                    pair = (tiles_ref[quarter, source, j], green_ref[:, pl.ds(start, side)])
                    terms.append((code // 256, lax.dot_general(
                        *(pair[::-1] if flipped else pair), (((1,), (1,)), ((), ())),
                        preferred_element_type=jnp.float32)))
            for aux, term in terms:
                total_ref[aux] += term

    core = lax.axis_index("row") % 2
    pl.when(core == 0)(lambda: add_all(False))
    pl.when(core == 1)(lambda: add_all(True))


def pair_kernel(total_hbm, chi_ref, total_ref, load_sem, right_in, left_in, done, occ_in, virt_in, plane_in, line_in,
                right_send, right_recv, left_send, left_recv, occ_send, occ_recv, virt_send, virt_recv,
                plane_send, plane_recv, line_send, line_recv):
    y, core, x, z = place()
    row = 2 * y + core
    count = total_ref.shape[0]
    rows = right_in.shape[1]
    thin = rows // 2
    steps = STEPS
    size = count // steps
    diagonal = x == y
    end = jnp.logical_or(z == 0, z == 3)

    def device(number):
        return (2 * (number // 4) + number % 2, (number // 2) % 2, z)

    mine = 4 * y + 2 * x + core
    load_total = pltpu.make_async_copy(total_hbm, total_ref, load_sem)
    load_total.start()
    barrier = pltpu.get_barrier_semaphore()
    for k in range(1, 4):
        pl.semaphore_signal(barrier, inc=1, device_id=(row, x, (z + k) % 4), device_id_type=MESH)
    for k in range(1, 8):
        pl.semaphore_signal(barrier, inc=1, device_id=device((mine + k) % 8), device_id_type=MESH)
    pl.semaphore_wait(barrier, 10)
    load_total.wait()

    def chunk(c):
        return pl.ds(c * size, size)

    def right(c, source):
        return pltpu.make_async_remote_copy(
            src_ref=source, dst_ref=right_in.at[chunk(c)], send_sem=right_send.at[c], recv_sem=right_recv.at[c],
            device_id=(row, x, (z + 1) % 4), device_id_type=MESH)

    def left(c, source):
        return pltpu.make_async_remote_copy(
            src_ref=source, dst_ref=left_in.at[chunk(c)], send_sem=left_send.at[c], recv_sem=left_recv.at[c],
            device_id=(row, x, (z + 3) % 4), device_id_type=MESH)

    def pass_right(c):
        right(c, right_in.at[chunk(c)]).wait_recv()
        right_in[chunk(c)] += total_ref[chunk(c), rows:]
        right(c, right_in.at[chunk(c)]).start()

    def pass_left(c):
        left(c, left_in.at[chunk(c)]).wait_recv()
        left_in[chunk(c)] += total_ref[chunk(c), :rows]
        left(c, left_in.at[chunk(c)]).start()

    def occ_copy(c):
        return pltpu.make_async_remote_copy(
            src_ref=done.at[chunk(c), thin:], dst_ref=occ_in.at[chunk(c)], send_sem=occ_send.at[c],
            recv_sem=occ_recv.at[c], device_id=(2 * y + 1 - core, x, z), device_id_type=MESH)

    def virt_copy(c, kk):
        return pltpu.make_async_remote_copy(
            src_ref=done.at[chunk(c), kk * thin:(kk + 1) * thin], dst_ref=virt_in.at[chunk(c)],
            send_sem=virt_send.at[c, kk], recv_sem=virt_recv.at[c], device_id=(2 * x + kk, y, z),
            device_id_type=MESH)

    def hand_out(c):
        @pl.when(core == 0)
        def _():
            occ_copy(c).start()
            occ_in[chunk(c)] = done[chunk(c), :thin]

        @pl.when(core == 1)
        def _():
            virt_copy(c, 0).start()

            @pl.when(diagonal)
            def _():
                virt_in[chunk(c)] = done[chunk(c), thin:]

            @pl.when(jnp.logical_not(diagonal))
            def _():
                virt_copy(c, 1).start()

    lag = 7

    @pl.when(z == 0)
    def _():
        for c in range(steps + lag):
            if c < steps:
                if c >= 5:
                    right(c - 5, total_ref.at[chunk(c - 5), rows:]).wait_send()
                right(c, total_ref.at[chunk(c), rows:]).start()
            if c >= lag:
                e = c - lag
                left(e, left_in.at[chunk(e)]).wait_recv()
                done[chunk(e)] = left_in[chunk(e)] + total_ref[chunk(e), :rows]
                hand_out(e)
        for c in range(steps - 5, steps):
            right(c, total_ref.at[chunk(c), rows:]).wait_send()

    @pl.when(z == 3)
    def _():
        for c in range(steps + lag):
            if c < steps:
                if c >= 5:
                    left(c - 5, total_ref.at[chunk(c - 5), :rows]).wait_send()
                left(c, total_ref.at[chunk(c), :rows]).start()
            if c >= lag:
                e = c - lag
                right(e, right_in.at[chunk(e)]).wait_recv()
                done[chunk(e)] = right_in[chunk(e)] + total_ref[chunk(e), rows:]
                hand_out(e)
        for c in range(steps - 5, steps):
            left(c, total_ref.at[chunk(c), :rows]).wait_send()

    def relay(near, far):
        for c in range(steps + 3):
            if c < steps:
                near(c)
            if c >= 3:
                far(c - 3)

    pl.when(z == 1)(lambda: relay(pass_right, pass_left))
    pl.when(z == 2)(lambda: relay(pass_left, pass_right))

    @pl.when(jnp.logical_not(end))
    def _():
        for c in range(steps):
            right(c, right_in.at[chunk(c)]).wait_send()
            left(c, left_in.at[chunk(c)]).wait_send()

    def plane(k):
        return pltpu.make_async_remote_copy(
            src_ref=plane_in.at[mine], dst_ref=plane_in.at[mine], send_sem=plane_send.at[k],
            recv_sem=plane_recv.at[k], device_id=device((mine + k) % 8), device_id_type=MESH)

    def line(which, k):
        return pltpu.make_async_remote_copy(
            src_ref=line_in.at[which], dst_ref=line_in.at[which], send_sem=line_send.at[k],
            recv_sem=line_recv.at[which], device_id=(row, x, (z + k) % 4), device_id_type=MESH)

    @pl.when(end)
    def _():
        for c in range(steps):
            @pl.when(core == 1)
            def _():
                occ_copy(c).wait_recv()

            @pl.when(jnp.logical_not(jnp.logical_and(diagonal, core == 1)))
            def _():
                virt_copy(c, 0).wait_recv()
        def halves(ref, i):
            values = jnp.concatenate([ref[:, i, :], ref[:, i + 1, :]], axis=1)
            high = values.astype(jnp.bfloat16)
            low = (values - high.astype(jnp.float32)).astype(jnp.bfloat16)
            return jnp.concatenate([high.astype(jnp.float32), low.astype(jnp.float32)], axis=0).astype(jnp.bfloat16)

        both = jnp.zeros((2 * count, 2 * count), jnp.float32)
        for i in range(0, thin, 2):
            both += lax.dot_general(halves(occ_in, i), halves(virt_in, i), (((1,), (1,)), ((), ())),
                                    preferred_element_type=jnp.float32)
        chi = (both[:count, :count] + both[count:, count:]) + (both[:count, count:] + both[count:, :count])
        plane_in[mine] = jnp.pad(chi, ((0, 0), (0, 128 - count)))
        for k in range(1, 8):
            plane(k).start()
        for k in range(1, 8):
            plane(k).wait_recv()
        summed = plane_in[0]
        for k in range(1, 8):
            summed += plane_in[k]

        @pl.when(z == 0)
        def _():
            line_in[0] = summed
            for k in (3, 2, 1):
                line(0, k).start()

        @pl.when(z == 3)
        def _():
            line_in[1] = summed
            for k in (1, 2, 3):
                line(1, k).start()

    @pl.when(z > 0)
    def _():
        line(0, 1).wait_recv()

    @pl.when(z < 3)
    def _():
        line(1, 1).wait_recv()

    chi_ref[...] = (line_in[0] + line_in[1])[:, :count]

    @pl.when(end)
    def _():
        for k in range(1, 8):
            plane(k).wait_send()
        for k in range(1, 4):
            line(0, k).wait_send()
        for c in range(steps):
            @pl.when(core == 0)
            def _():
                occ_copy(c).wait_send()

            @pl.when(core == 1)
            def _():
                virt_copy(c, 0).wait_send()

                @pl.when(jnp.logical_not(diagonal))
                def _():
                    virt_copy(c, 1).wait_send()


def on_slice(blocks, block_aux, block_row, block_col, extents, occ_green, virt_green):
    held, side, _ = blocks.shape
    owners = 8
    cap = held // owners + 1
    depth, width = occ_green.shape
    smem, vmem = pl.BlockSpec(memory_space=pltpu.SMEM), pl.BlockSpec(memory_space=pltpu.VMEM)
    f32, i32 = jnp.float32, jnp.int32
    dma = pltpu.SemaphoreType.DMA

    def bind(kernel, *sizes):
        def run(*refs):
            kernel(*sizes, *refs)
        return run

    lists = jnp.pad(jnp.stack([block_aux, block_row, block_col, extents]), ((0, 4), (0, 128 - held)),
                    constant_values=1 << 20)
    part = cap // 4
    tiles, meta, green = pl.pallas_call(
        bind(exchange_kernel, cap, depth // side),
        out_shape=(
            jax.ShapeDtypeStruct((4, owners, part, side, side), blocks.dtype),
            jax.ShapeDtypeStruct((owners, 8, 128), i32),
            jax.ShapeDtypeStruct((2 * width, depth), occ_green.dtype),
        ),
        in_specs=[pl.BlockSpec(memory_space=pl.ANY)] * 4,
        out_specs=(vmem, vmem, vmem),
        scratch_shapes=[
            pltpu.VMEM(blocks.shape, blocks.dtype),
            pltpu.VMEM((width, depth), occ_green.dtype),
            pltpu.VMEM((8, 128), i32),
            pltpu.VMEM((8, 128), i32),
            pltpu.SMEM((8, 128), i32),
            pltpu.VMEM((owners, 8, 128), i32),
            pltpu.VMEM((7, part, side, side), blocks.dtype),
            dma((5,)),
            dma((7,)), dma((7,)), dma((7,)), dma((7,)), dma((8,)), dma((8,)), dma((16,)), dma((16,)),
            dma(()), dma(()),
        ],
        compiler_params=pltpu.CompilerParams(collective_id=0, has_side_effects=True, vmem_limit_bytes=VMEM_LIMIT),
        name="exchange",
    )(lists, blocks, occ_green.T, virt_green.T)
    total = pl.pallas_call(
        bind(product_kernel, cap),
        out_shape=jax.ShapeDtypeStruct((NP, side, 2 * width), f32),
        in_specs=[smem, pl.BlockSpec(memory_space=pl.ANY), pl.BlockSpec(memory_space=pl.ANY)],
        out_specs=vmem,
        scratch_shapes=[
            pltpu.VMEM((4, owners, part, side, side), blocks.dtype),
            pltpu.VMEM((2 * width, depth), occ_green.dtype),
            dma((5,)),
        ],
        compiler_params=pltpu.CompilerParams(vmem_limit_bytes=VMEM_LIMIT),
        name="product",
    )(meta, tiles, green)
    rows, part_rows = side // 2, side // 4
    return pl.pallas_call(
        pair_kernel,
        out_shape=jax.ShapeDtypeStruct((NP, NP), f32),
        in_specs=[pl.BlockSpec(memory_space=pl.ANY)],
        out_specs=vmem,
        scratch_shapes=[
            pltpu.VMEM((NP, side, side), f32),
            dma(()),
            pltpu.VMEM((NP, rows, side), f32),
            pltpu.VMEM((NP, rows, side), f32),
            pltpu.VMEM((NP, rows, side), f32),
            pltpu.VMEM((NP, part_rows, side), f32),
            pltpu.VMEM((NP, part_rows, side), f32),
            pltpu.VMEM((8, NP, 128), f32),
            pltpu.VMEM((2, NP, 128), f32),
            dma((STEPS,)), dma((STEPS,)), dma((STEPS,)), dma((STEPS,)), dma((STEPS,)), dma((STEPS,)),
            dma((STEPS, 2)), dma((STEPS,)), dma((8,)), dma((8,)), dma((4,)), dma((2,)),
        ],
        compiler_params=pltpu.CompilerParams(collective_id=1, has_side_effects=True, vmem_limit_bytes=53 * 1024 * 1024),
        name="pair",
    )(total)


def on_device(blocks, block_aux, block_row, block_col, extents, occ_green, virt_green):
    row_count = lax.axis_size("row")
    col_count = lax.axis_size("col")
    layer_count = lax.axis_size("layer")
    held_count = blocks.shape[0]
    tile_side = blocks.shape[1]
    aux_count = NP
    owner_count = col_count * layer_count
    capacity = max(2, held_count // owner_count + 1)
    layer_blocks = occ_green.shape[0] // tile_side
    columns = jnp.arange(tile_side, dtype=jnp.int32)
    masked_tiles = jnp.where(
        columns[None, None, :] < extents[:, None, None], blocks, jnp.zeros((), blocks.dtype)
    )
    layer_of = block_col // layer_blocks
    target = block_row * layer_count + layer_of
    kept_col = block_col - layer_of * layer_blocks
    marked = (target[:, None] == jnp.arange(owner_count, dtype=jnp.int32)[None, :]).astype(
        jnp.int32
    )
    earlier = jnp.cumsum(marked, axis=0) - marked
    placed = target * capacity + jnp.sum(earlier * marked, axis=1)
    send_tiles = (
        jnp.zeros((owner_count * capacity, tile_side, tile_side), blocks.dtype)
        .at[placed]
        .set(masked_tiles)
    )
    send_meta = (
        jnp.zeros((owner_count * capacity, 2), jnp.int32)
        .at[placed]
        .set(jnp.stack([block_aux, kept_col], axis=1))
    )
    send_tiles = send_tiles.reshape(col_count, layer_count, capacity, tile_side, tile_side)
    send_meta = send_meta.reshape(col_count, layer_count, capacity, 2)
    total_slots = col_count * layer_count * capacity
    got_tiles, got_meta = (
        lax.all_to_all(
            send_tiles.reshape(total_slots, tile_side, tile_side),
            ("col", "layer"),
            split_axis=0,
            concat_axis=0,
            tiled=True,
        ),
        lax.all_to_all(
            send_meta.reshape(total_slots, 2),
            ("col", "layer"),
            split_axis=0,
            concat_axis=0,
            tiled=True,
        ),
    )
    group_size = col_count * capacity
    got_tiles = got_tiles.reshape(layer_count, group_size, tile_side, tile_side)
    got_meta = got_meta.reshape(layer_count, group_size, 2)
    occ_cols, virt_cols = (occ_green, virt_green)
    width_here = occ_cols.shape[1]
    offsets = jnp.arange(tile_side, dtype=jnp.int32)

    def add_group(totals, record):
        occ_total, virt_total = totals
        tile_group, meta_group = record
        row_index = meta_group[:, 1][:, None] * tile_side + offsets[None, :]
        occ_rows = occ_cols[row_index]
        virt_rows = virt_cols[row_index]
        occ_term = jnp.einsum(
            "gsv,gls->gvl", occ_rows, tile_group, preferred_element_type=jnp.float32
        )
        virt_term = jnp.einsum(
            "gvs,gsl->gvl", tile_group, virt_rows, preferred_element_type=jnp.float32
        )
        aux_index = meta_group[:, 0]
        return (
            (occ_total.at[aux_index].add(occ_term), virt_total.at[aux_index].add(virt_term)),
            None,
        )

    start_totals = (
        jnp.zeros((aux_count, width_here, tile_side), jnp.float32),
        jnp.zeros((aux_count, tile_side, width_here), jnp.float32),
    )
    (occ_total, virt_total), _ = lax.scan(add_group, start_totals, (got_tiles, got_meta))
    occ_done, virt_done = (
        lax.psum_scatter(occ_total, "layer", scatter_dimension=1, tiled=True),
        lax.psum_scatter(virt_total, "layer", scatter_dimension=2, tiled=True),
    )
    mesh_count = row_count * layer_count
    thin_rows = tile_side // mesh_count
    stack_count = mesh_count // col_count
    narrow = occ_done.shape[1]
    occ_five = occ_done.reshape(aux_count, 1, col_count, thin_rows, tile_side)
    virt_five = virt_done.reshape(aux_count, stack_count, col_count, thin_rows, narrow)
    occ_moved, virt_moved = (
        lax.all_to_all(occ_five, "col", split_axis=2, concat_axis=1, tiled=True),
        lax.all_to_all(virt_five, "col", split_axis=2, concat_axis=1, tiled=True),
    )
    virt_four = virt_moved.reshape(aux_count, mesh_count, thin_rows, narrow)
    virt_back = lax.all_to_all(virt_four, ("row", "layer"), split_axis=1, concat_axis=3, tiled=True)
    occ_final = occ_moved.reshape(aux_count, col_count, thin_rows, tile_side)
    virt_final = virt_back.reshape(aux_count, thin_rows, col_count, tile_side)
    chi_part = jnp.einsum(
        "pcji,qjci->pq",
        occ_final,
        virt_final,
        precision=lax.Precision.HIGHEST,
        preferred_element_type=jnp.float32,
    )
    return lax.psum(chi_part, ("row", "col", "layer"))


def solution(mesh):
    in_specs = (
        P(("col", "layer"), None, None),
        P(("col", "layer")),
        P(("col", "layer")),
        P(("col", "layer")),
        P(("col", "layer")),
        P("layer", "row"),
        P("layer", "row"),
    )
    out_specs = P()
    side_of = (mesh.shape["row"], mesh.shape["col"], mesh.shape["layer"])
    return jax.shard_map(
        on_slice if side_of == (4, 2, 4) else on_device, mesh=mesh, in_specs=in_specs, out_specs=out_specs, check_vma=False
    )
```
